256 devices in a mesh: seq: 64 (over y, x_lo, z), head: 4 (over x_hi, core).
Axes of the slice: x: 4 (x_hi: 2, x_lo: 2; x = x_hi * 2 + x_lo), y: 4, z: 8, core: 2. Of those that a mesh axis runs over, the one named last changes fastest.
Arguments:
- queries: bfloat16 [32768, 2560], P('seq', 'head'), may hold values from -150 to 150
- keys: bfloat16 [32768, 2560], P('seq', 'head'), may hold values from -6 to 6
- values_in: bfloat16 [32768, 2560], P('seq', 'head'), may hold values from -6 to 6
- cotangent: bfloat16 [32768, 2560], P('seq', 'head'), may hold values from -6 to 6
- w_value: float32 [2560], P('head'), may hold values from -6 to 6
- returns: float32 [32768], P('seq'), may hold values from -8 to 8
Outputs:
- critic_values: float32 [32768], P('seq')
- grad_w_value: float32 [2560], P('head')
- grad_queries: bfloat16 [32768, 2560], P('seq', 'head')
- grad_keys: bfloat16 [32768, 2560], P('seq', 'head')
- grad_values: bfloat16 [32768, 2560], P('seq', 'head')
The draws below stay inside these ranges and needn't reach their ends.
All inputs are finite; a program needn't handle non-finite values.
Results may differ from the reference program's by a relative error of at most 0.013.
Values may be sent and summed in bfloat16 or wider, within the bound.
No kernel may reach another device: no remote copies, remote signals or barrier semaphores. Data moves between devices by JAX's collectives and lax.ppermute only.
A program may use at most 128 MiB of HBM per device.

```python
import jax
import jax.numpy as jnp
from jax import lax

HEADS = 20
HSZ = 128
STRIDE = 512
TOK_DEV = 512
TOKENS = 32768


def key_base(key):
    return jnp.clip(jax.random.normal(key, (TOKENS, HEADS * HSZ), jnp.float32), -6.0, 6.0)


def draw_keys(key, part):
    base = key_base(key)
    return base.astype(jnp.bfloat16)


def draw_queries(key, part):
    key = jax.random.fold_in(key, 7)
    fresh = jnp.clip(jax.random.normal(key, (TOKENS, HEADS * HSZ), jnp.float32), -6.0, 6.0)
    return fresh.astype(jnp.bfloat16)


def shard_levels(rng, extent, shards, low, top_value):
    gain, own = 1.0, jax.random.fold_in(rng, 6)
    for dim, shards_of in shards:
        steps = jnp.exp(jax.random.uniform(jax.random.fold_in(own, dim), (shards_of,), jnp.float32, low / len(shards), top_value / len(shards)))
        gain = gain * jnp.repeat(steps, extent[dim] // shards_of).reshape([-1 if axis == dim else 1 for axis in range(len(extent))])
    return gain


def scatter_about(stream_key, dims, width, limit, split=(), held_as=jnp.bfloat16):
    array = jax.random.normal(stream_key, dims, jnp.float32) * width
    if len(split) > 0:
        array = shard_levels(stream_key, dims, split, -0.22, 0.18) * array
    return jnp.clip(array, min=-limit, max=limit).astype(held_as)


def setup_inputs(seed: int = 0) -> dict:
    splits = jax.random.split(jax.random.key(seed), 7)
    return {
        "queries": draw_queries(jax.random.fold_in(splits[6], 71), 0),
        "keys": draw_keys(jax.random.fold_in(splits[6], 71), 0),
        "values_in": scatter_about(splits[2], (TOKENS, HEADS * HSZ), 1.0, 6.0, ((0, 64), (1, 4))),
        "cotangent": scatter_about(splits[3], (TOKENS, HEADS * HSZ), 1.0, 6.0, ((0, 64), (1, 4))),
        "w_value": scatter_about(splits[4], (HEADS * HSZ,), 1.0, 6.0, ((0, 4),), jnp.float32),
        "returns": scatter_about(splits[5], (TOKENS,), 2.0, 8.0, ((0, 64),), jnp.float32),
    }


def roundtrip(x):
    return lax.optimization_barrier(x.astype(jnp.bfloat16)).astype(jnp.float32)


def reference(queries, keys, values_in, cotangent, w_value, returns):
    span = STRIDE
    blocks = TOKENS // span
    periods = TOK_DEV // span
    scale = HSZ ** -0.5
    shape4 = (blocks, span, HEADS, HSZ)
    q4 = queries.reshape(shape4)
    k4 = keys.reshape(shape4)
    v4 = values_in.reshape(shape4)
    zero = jnp.zeros((1, span, HEADS, HSZ), jnp.bfloat16)
    kprev = jnp.concatenate([zero, k4[:-1]], axis=0)
    vprev = jnp.concatenate([zero, v4[:-1]], axis=0)
    rowa = jnp.arange(span)[:, None]
    colb = jnp.arange(2 * span)[None, :]
    base_valid = (colb > rowa) & (colb <= span + rowa)
    first = jnp.arange(blocks) == 0

    def row_scores(qb, kp, ko, fst):
        kk = jnp.concatenate([kp, ko], axis=0)
        valid = base_valid & ((colb >= span) | jnp.logical_not(fst))
        s = jnp.einsum('ahe,bhe->hab', qb.astype(jnp.float32), kk.astype(jnp.float32)) * scale
        return s, valid[None], kk

    def row_fwd(args):
        qb, kp, ko, vp, vo, fst = args
        s, valid, kk = row_scores(qb, kp, ko, fst)
        vv = jnp.concatenate([vp, vo], axis=0)
        m = jnp.max(jnp.where(valid, s, -1e30), axis=2, keepdims=True)
        pr = jnp.where(valid, jnp.exp(s - m), 0.0)
        tot = jnp.sum(pr, axis=2)
        num = jnp.einsum('hab,bhe->ahe', pr.astype(jnp.bfloat16).astype(jnp.float32), vv.astype(jnp.float32))
        return num / tot.T[:, :, None], (m[:, :, 0] + jnp.log(tot)).T

    o_r, lse_r = lax.map(row_fwd, (q4, kprev, k4, vprev, v4, first))

    pidx = jnp.arange(blocks)
    cvalid = (pidx[:, None] > pidx[None, :])[None, None]
    has = pidx >= 1
    sc = jnp.einsum('pohe,qohe->ohpq', q4.astype(jnp.float32), k4.astype(jnp.float32)) * scale
    mc = jnp.max(jnp.where(cvalid, sc, -1e30), axis=3, keepdims=True)
    pc = jnp.where(cvalid, jnp.exp(sc - mc), 0.0)
    totc = jnp.sum(pc, axis=3)
    safe = jnp.where(has[None, None], totc, 1.0)
    numc = jnp.einsum('ohpq,qohe->pohe', pc.astype(jnp.bfloat16).astype(jnp.float32), v4.astype(jnp.float32))
    o_c = (numc / safe.transpose(2, 0, 1)[..., None]).astype(jnp.bfloat16)
    lse_c = jnp.where(has[None, None], mc[..., 0] + jnp.log(safe), -1e30).transpose(2, 0, 1)

    lse = jnp.logaddexp(lse_r, lse_c)
    out = jnp.exp(lse_r - lse)[..., None] * o_r + jnp.exp(lse_c - lse)[..., None] * o_c.astype(jnp.float32)
    outflat = out.reshape(TOKENS, HEADS * HSZ)
    critic_values = jnp.sum(outflat * w_value[None, :], axis=1)
    resid = critic_values - returns
    grad_w_value = jnp.sum(resid[:, None] * outflat, axis=0)
    dout = (cotangent.astype(jnp.float32) + resid[:, None] * w_value[None, :]).astype(jnp.bfloat16)
    do4 = dout.reshape(shape4)
    dsum = jnp.sum(do4.astype(jnp.float32) * out, axis=3)

    def row_bwd(args):
        qb, kp, ko, vp, vo, fst, dob, lb, db = args
        s, valid, kk = row_scores(qb, kp, ko, fst)
        vv = jnp.concatenate([vp, vo], axis=0)
        pr = jnp.where(valid, jnp.exp(s - lb.T[:, :, None]), 0.0)
        dof = dob.astype(jnp.float32)
        dv = jnp.einsum('hab,ahe->bhe', pr.astype(jnp.bfloat16).astype(jnp.float32), dof)
        dp = jnp.einsum('ahe,bhe->hab', dof, vv.astype(jnp.float32))
        ds = (pr * (dp - db.T[:, :, None])).astype(jnp.bfloat16).astype(jnp.float32)
        dq = scale * jnp.einsum('hab,bhe->ahe', ds, kk.astype(jnp.float32))
        dk = scale * jnp.einsum('hab,ahe->bhe', ds, qb.astype(jnp.float32))
        return dq, dk[:span], dk[span:], dv[:span], dv[span:]

    dq_r, dk_p, dk_o, dv_p, dv_o = lax.map(row_bwd, (q4, kprev, k4, vprev, v4, first, do4, lse, dsum))

    lt = lse.transpose(1, 2, 0)[..., None]
    dt = dsum.transpose(1, 2, 0)[..., None]
    pcb = jnp.where(cvalid, jnp.exp(sc - lt), 0.0)
    dof4 = do4.astype(jnp.float32)
    dv_c = jnp.einsum('ohpq,pohe->qohe', pcb.astype(jnp.bfloat16).astype(jnp.float32), dof4)
    dpc = jnp.einsum('pohe,qohe->ohpq', dof4, v4.astype(jnp.float32))
    dsc = (pcb * (dpc - dt)).astype(jnp.bfloat16).astype(jnp.float32)
    dq_c = scale * jnp.einsum('ohpq,qohe->pohe', dsc, k4.astype(jnp.float32))
    dk_c = scale * jnp.einsum('ohpq,pohe->qohe', dsc, q4.astype(jnp.float32))

    boundary = (((jnp.arange(blocks) + 1) % periods) == 0)[:, None, None, None]
    pad = jnp.zeros((1, span, HEADS, HSZ), jnp.float32)

    def cross(part):
        nxt = jnp.concatenate([part[1:], pad], axis=0)
        return jnp.where(boundary, roundtrip(nxt), nxt)

    grad_q = (dq_r + roundtrip(dq_c)).astype(jnp.bfloat16).reshape(TOKENS, HEADS * HSZ)
    grad_k = (dk_o + cross(dk_p) + roundtrip(dk_c)).astype(jnp.bfloat16).reshape(TOKENS, HEADS * HSZ)
    grad_v = (dv_o + cross(dv_p) + roundtrip(dv_c)).astype(jnp.bfloat16).reshape(TOKENS, HEADS * HSZ)
    return (critic_values, grad_w_value, grad_q, grad_k, grad_v)
```

```python
import functools

import jax
import jax.numpy as jnp
from jax import lax
from jax.experimental import pallas as pl
from jax.experimental.pallas import tpu as pltpu
from jax.sharding import PartitionSpec as P

HSZ = 128
STRIDE = 512
NH = 5
POS = 64
OFF = 8
QB = 256
NEG = -1e30
SCALE = HSZ ** (-0.5)
VMEM = 60 * 1024 * 1024
F32 = jnp.float32
BF16 = jnp.bfloat16


def iota(shape, dim):
    return lax.broadcasted_iota(jnp.int32, shape, dim)


def dot_nt(a, b):
    return lax.dot_general(a, b, (((1,), (1,)), ((), ())), preferred_element_type=F32)


def dot_nn(a, b):
    return lax.dot_general(a, b, (((1,), (0,)), ((), ())), preferred_element_type=F32)


def dot_tn(a, b):
    return lax.dot_general(a, b, (((0,), (0,)), ((), ())), preferred_element_type=F32)


def exact(a, b, dims):
    return lax.dot_general(
        a, b, (dims, ((), ())), preferred_element_type=F32, precision=lax.Precision.HIGHEST
    )


def pack(r):
    spread = (iota((16, 128), 1) // OFF == iota((16, 128), 0)).astype(F32)
    a = exact(r, spread, ((0,), (0,)))
    a = jnp.where(iota((512, 128), 0) % OFF == iota((512, 128), 1) % OFF, a, 0.0)
    gather = (iota((POS, 512), 1) // OFF == iota((POS, 512), 0)).astype(F32)
    return exact(gather, a, ((1,), (0,)))


def unpack(m):
    spread = (iota((512, POS), 0) // OFF == iota((512, POS), 1)).astype(F32)
    a = exact(spread, m, ((1,), (0,)))
    a = jnp.where(iota((512, 128), 0) % OFF == iota((512, 128), 1) % OFF, a, 0.0)
    gather = (iota((16, 128), 1) // OFF == iota((16, 128), 0)).astype(F32)
    return exact(gather, a, ((1,), (1,)))


def split3(x):
    hi = x.astype(BF16)
    rest = x - hi.astype(F32)
    mid = rest.astype(BF16)
    return hi, mid, (rest - mid.astype(F32)).astype(BF16)


def resid_columns(resid):
    hi, mid, lo = split3(resid)
    rows = jnp.concatenate([hi, mid, lo, jnp.zeros((13, 512), BF16)], axis=0)
    eye = (iota((16, 128), 0) == iota((16, 128), 1)).astype(BF16)
    return dot_tn(rows, eye).astype(BF16)


def col_bias():
    key, query = iota((QB, QB), 0), iota((QB, QB), 1)
    same = key % OFF == query % OFF
    below = jnp.where(same, 0.0, NEG).astype(F32)
    diag = jnp.where(same & (key // OFF < query // OFF), 0.0, NEG).astype(F32)
    return diag, below


def col_scores(k, q, masks, qb):
    diag, below = masks
    s = dot_nt(k[0 : (qb + 1) * QB], q[qb * QB : (qb + 1) * QB])
    return [s[i * QB : (i + 1) * QB] + (diag if i == qb else below) for i in range(qb + 1)]


def rsum(x):
    return jnp.sum(x, axis=0, keepdims=True)


def stats_of(s, dp, wv):
    top = functools.reduce(jnp.maximum, [jnp.max(x, axis=0, keepdims=True) for x in s])
    e = [jnp.exp((x - top) * SCALE) for x in s]
    z = sum(rsum(x) for x in e)
    u = sum(rsum(x * y) for x, y in zip(e, wv))
    c = sum(rsum(x * y) for x, y in zip(e, dp))
    return top * SCALE + jnp.log(z), u / z, c / z, z, e


def wv_of(v, w):
    return jnp.sum(v.astype(F32) * w, axis=1, keepdims=True)


def row_window(kp_ref, k_ref, qb):
    runs = [kp_ref[0:QB, :], kp_ref[QB:, :], k_ref[0:QB, :], k_ref[QB:, :]]
    return jnp.concatenate(runs[qb : qb + 3], axis=0)


def upper():
    return iota((QB, QB), 0) > iota((QB, QB), 1)


def row_scores(kw, q, bias, qb):
    s = dot_nt(kw, q)
    up = upper()
    s0 = jnp.where(up, s[0:QB], NEG) + bias
    s1 = s[QB : 2 * QB]
    if qb == 0:
        s1 = s1 + bias
    s2 = jnp.where(up, NEG, s[2 * QB :])
    return jnp.concatenate([s0, s1, s2], axis=0)


def row_fwd_kernel(
    bias_ref, q_ref, kp_ref, k_ref, vp_ref, v_ref, c_ref, w_ref, ret_ref, nat_ref, pack_ref, o_ref, st_ref
):
    h = pl.program_id(0)
    w = w_ref[0:1, :]
    bias = bias_ref[0]
    for qb in range(2):
        at = slice(qb * QB, (qb + 1) * QB)
        kw = row_window(kp_ref, k_ref, qb)
        vw = row_window(vp_ref, v_ref, qb)
        s = row_scores(kw, q_ref[at, :], bias, qb)
        dp = dot_nt(vw, c_ref[at, :])
        lse, u, c, z, e = stats_of([s], [dp], [wv_of(vw, w)])
        o_ref[at, :] = dot_tn(e[0].astype(BF16), vw).astype(BF16)
        st_ref[h, :, at] = jnp.concatenate([lse, u, c, z, z, z, z, z], axis=0)

    @pl.when(h == NH - 1)
    def _():
        r = jnp.concatenate([st_ref[:, i, :] for i in range(3)] + [ret_ref[0:1, :]], axis=0)
        nat_ref[0:16, :] = r
        nat_ref[16:21, :] = st_ref[:, 3, :]
        nat_ref[21:24, :] = jnp.zeros((3, STRIDE), F32)
        pack_ref[...] = pack(r)


def col_fwd_kernel(g_ref, w_ref, pack_ref, nat_ref, out_ref):
    masks = col_bias()
    has = iota((1, STRIDE), 1) >= OFF
    rows = [[], [], []]
    for h in range(NH):
        q, k, v, c = (g_ref[:, (i * NH + h) * HSZ : (i * NH + h + 1) * HSZ] for i in range(4))
        wv = wv_of(v, w_ref[0:1, h * HSZ : (h + 1) * HSZ])
        parts = []
        for qb in range(2):
            s = col_scores(k, q, masks, qb)
            dp = dot_nt(v[0 : (qb + 1) * QB], c[qb * QB : (qb + 1) * QB])
            cut = [slice(i * QB, (i + 1) * QB) for i in range(qb + 1)]
            parts.append(stats_of(s, [dp[x] for x in cut], [wv[x] for x in cut])[0:3])
        for i in range(3):
            row = jnp.concatenate([parts[0][i], parts[1][i]], axis=1)
            rows[i].append(jnp.where(has, row, NEG if i == 0 else 0.0))
    r = jnp.concatenate(rows[0] + rows[1] + rows[2] + [jnp.zeros((1, STRIDE), F32)], axis=0)
    nat_ref[...] = r
    out_ref[:, 0, :] = pack_ref[...]
    out_ref[:, 1, :] = pack(r)


def merge(r, c):
    lse_r, lse_c = r[0:5], c[0:5]
    top = jnp.maximum(lse_r, lse_c)
    lse = top + jnp.log(jnp.exp(lse_r - top) + jnp.exp(lse_c - top))
    a_r, a_c = jnp.exp(lse_r - lse), jnp.exp(lse_c - lse)
    u = a_r * r[5:10] + a_c * c[5:10]
    cc = a_r * r[10:15] + a_c * c[10:15]
    return jnp.concatenate([lse, u, cc, r[15:16]], axis=0), jnp.sum(u, axis=0, keepdims=True), a_r


def merge_kernel(rnat_ref, cnat_ref, got_ref, t_ref, tc_ref, part_ref):
    nat = rnat_ref[...]
    t, part, a_r = merge(nat[0:16], unpack(got_ref[:, 1, :]))
    t_ref[0:16, :] = t
    t_ref[16:21, :] = a_r / nat[16:21]
    t_ref[21:24, :] = jnp.zeros((3, STRIDE), F32)
    tc, partc, _ = merge(unpack(got_ref[:, 0, :]), cnat_ref[...])
    tc_ref[...] = tc
    part_ref[...] = jnp.concatenate([part, partc, jnp.zeros((6, STRIDE), F32)], axis=0)


def resid_of(t_ref, crit_ref, role):
    return crit_ref[role : role + 1, :] - t_ref[15:16, :]


def bwd_lanes(t_ref, resid, h):
    lse = t_ref[pl.ds(h, 1), :]
    u = t_ref[pl.ds(NH + h, 1), :]
    c = t_ref[pl.ds(2 * NH + h, 1), :]
    return lse, c + resid * u


def grads(s, dp, wv, lse, resid, dsum):
    p = jnp.exp(s * SCALE - lse)
    g = p * (dp + (wv * resid - dsum))
    return p.astype(BF16), g.astype(BF16)


def col_bwd_kernel(g_ref, w_ref, tc_ref, t_ref, crit_ref, o_ref, out_ref, dv_ref, dk_ref):
    masks = col_bias()
    resid = resid_of(tc_ref, crit_ref, 1)
    rc = resid_columns(resid)
    resid_r = resid_of(t_ref, crit_ref, 0)
    gws = []
    for h in range(NH):
        q, k, v, c = (g_ref[:, (i * NH + h) * HSZ : (i * NH + h + 1) * HSZ] for i in range(4))
        w = w_ref[0:1, h * HSZ : (h + 1) * HSZ]
        wv = wv_of(v, w)
        lse, dsum = bwd_lanes(tc_ref, resid, h)
        at_q, at_k, at_v = (slice((3 * h + i) * HSZ, (3 * h + i + 1) * HSZ) for i in range(3))
        for qb in range(2):
            at = slice(qb * QB, (qb + 1) * QB)
            rows = (qb + 1) * QB
            s = jnp.concatenate(col_scores(k, q, masks, qb), axis=0)
            dp = dot_nt(v[0:rows], c[at])
            p, g = grads(s, dp, wv[0:rows], lse[:, at], resid[:, at], dsum[:, at])
            dv = dot_nn(p, jnp.concatenate([c[at], rc[at]], axis=1))
            dk = dot_nn(g, q[at])
            out_ref[at, at_q] = (dot_tn(g, k[0:rows]) * SCALE).astype(BF16)
            if qb == 0:
                dv_ref[...] = dv
                dk_ref[...] = dk
            else:
                dv = jnp.concatenate([dv[0:QB] + dv_ref[...], dv[QB:]], axis=0)
                dk = jnp.concatenate([dk[0:QB] + dk_ref[...], dk[QB:]], axis=0)
        cj = jnp.sum(dv[:, HSZ:], axis=1, keepdims=True)
        out_ref[:, at_k] = (dk * SCALE).astype(BF16)
        out_ref[:, at_v] = (dv[:, 0:HSZ] + cj * w).astype(BF16)
        gw = rsum(cj * v.astype(F32))
        weight = jnp.concatenate(split3(resid_r * t_ref[16 + h : 17 + h, :]) + (jnp.zeros((13, STRIDE), BF16),), axis=0)
        gws.append(gw + rsum(dot_nn(weight, o_ref[:, h * HSZ : (h + 1) * HSZ])))
    tile = jnp.concatenate(gws + [jnp.zeros((3, HSZ), F32)], axis=0)
    tile = jnp.broadcast_to(tile[None], (POS, OFF, HSZ)).reshape(STRIDE, HSZ)
    out_ref[:, 3 * NH * HSZ :] = tile.astype(BF16)


def row_bwd_kernel(
    bias_ref, q_ref, qn_ref, kp_ref, k_ref, vp_ref, v_ref, c_ref, cn_ref, w_ref, t_ref, tn_ref, crit_ref, critn_ref,
    out_ref, rc_ref, dv_ref, dk_ref,
):
    h = pl.program_id(0)
    resid = resid_of(t_ref, crit_ref, 0)
    resid_n = resid_of(tn_ref, critn_ref, 0)

    @pl.when(h == 0)
    def _():
        rc_ref[0] = resid_columns(resid)
        rc_ref[1] = resid_columns(resid_n)

    lse, dsum = bwd_lanes(t_ref, resid, h)
    lse_n, dsum_n = bwd_lanes(tn_ref, resid_n, h)
    w = w_ref[0:1, :]
    wv = wv_of(v_ref[...], w)
    wvp = wv_of(vp_ref[...], w)
    wvx = jnp.concatenate([wvp, wv], axis=0)
    for qb in range(2):
        at = slice(qb * QB, (qb + 1) * QB)
        kw = row_window(kp_ref, k_ref, qb)
        vw = row_window(vp_ref, v_ref, qb)
        s = row_scores(kw, q_ref[at, :], bias_ref[0], qb)
        dp = dot_nt(vw, c_ref[at, :])
        p, g = grads(s, dp, wvx[qb * QB : (qb + 3) * QB], lse[:, at], resid[:, at], dsum[:, at])
        out_ref[at, 0:HSZ] = dot_tn(g, kw) * SCALE
        own = (2 - qb) * QB
        caug = jnp.concatenate([c_ref[at, :], rc_ref[0, at, :]], axis=1)
        dv = dot_nn(p[own:], caug)
        dk = dot_nn(g[own:], q_ref[at, :])
        if qb == 0:
            dv_ref[0:QB, :] = dv
            dk_ref[0:QB, :] = dk
        else:
            dv_ref[0:QB, :] += dv[0:QB]
            dk_ref[0:QB, :] += dk[0:QB]
            dv_ref[QB:, :] = dv[QB:]
            dk_ref[QB:, :] = dk[QB:]
    up = upper()
    for qb in range(2):
        at = slice(qb * QB, (qb + 1) * QB)
        kw, vw = k_ref[qb * QB :, :], v_ref[qb * QB :, :]
        s = dot_nt(kw, qn_ref[at, :]) + bias_ref[1]
        s0 = jnp.where(up, s[0:QB], NEG)
        s = jnp.concatenate([s0, s[QB:]], axis=0) if qb == 0 else s0
        dp = dot_nt(vw, cn_ref[at, :])
        p, g = grads(s, dp, wv[qb * QB :], lse_n[:, at], resid_n[:, at], dsum_n[:, at])
        caug = jnp.concatenate([cn_ref[at, :], rc_ref[1, at, :]], axis=1)
        dv_ref[qb * QB :, :] += dot_nn(p, caug)
        dk_ref[qb * QB :, :] += dot_nn(g, qn_ref[at, :])
    cj = jnp.sum(dv_ref[:, HSZ:], axis=1, keepdims=True)
    out_ref[:, HSZ : 2 * HSZ] = dk_ref[...] * SCALE
    out_ref[:, 2 * HSZ :] = dv_ref[:, 0:HSZ] + cj * w


def final_kernel(row_ref, col_ref, q_ref, k_ref, v_ref, gw_ref):
    step = pl.program_id(0)
    for h in range(NH):
        for i, ref in enumerate((q_ref, k_ref, v_ref)):
            at = slice((3 * h + i) * HSZ, (3 * h + i + 1) * HSZ)
            ref[:, h * HSZ : (h + 1) * HSZ] = (row_ref[:, at] + col_ref[:, at].astype(F32)).astype(BF16)
    tiles = col_ref[:, 3 * NH * HSZ :].astype(F32)
    tile = jnp.sum(tiles.reshape(tiles.shape[0] // OFF, OFF, HSZ), axis=0)

    @pl.when(step == 0)
    def _():
        gw_ref[...] = tile

    @pl.when(step > 0)
    def _():
        gw_ref[...] += tile


def heads(at=0, rows=STRIDE, width=HSZ):
    return pl.BlockSpec((rows, width), lambda h: (0, at + h))


def whole(*shape):
    return pl.BlockSpec(shape, lambda h: (0,) * len(shape))


SMEM = pl.BlockSpec(memory_space=pltpu.SMEM)
PARAMS = pltpu.CompilerParams(vmem_limit_bytes=VMEM, dimension_semantics=("arbitrary",))


def shape(*dims, dtype=F32):
    return jax.ShapeDtypeStruct(dims, dtype)


def call(kernel, ins, outs, out_shape, scratch=(), name=None):
    return pl.pallas_call(
        kernel,
        grid=(NH,),
        in_specs=ins,
        out_specs=outs,
        out_shape=out_shape,
        scratch_shapes=list(scratch),
        compiler_params=PARAMS,
        name=name,
    )


def single(kernel, out_shape, scratch=(), name=None):
    return pl.pallas_call(
        kernel,
        out_shape=out_shape,
        scratch_shapes=list(scratch),
        compiler_params=pltpu.CompilerParams(vmem_limit_bytes=VMEM),
        name=name,
    )


def doubling(x, axis, steps):
    n = lax.axis_size(axis)
    for step in steps:
        x = x + lax.ppermute(x, axis, [(i, i ^ step) for i in range(n)])
    return x


def body(queries, keys, values_in, cotangent, w_value, returns):
    seq = lax.axis_size("seq")
    at = lax.axis_index("seq")
    bias = jnp.where(jnp.stack([at == 0, at == seq - 1]), NEG, 0.0).astype(F32)
    w8 = jnp.broadcast_to(w_value[None, :], (8, w_value.shape[0]))
    ret8 = jnp.broadcast_to(returns[None, :], (8, STRIDE))

    ahead = [(i, i + 1) for i in range(seq - 1)]
    behind = [(i + 1, i) for i in range(seq - 1)]
    prev_k = lax.ppermute(keys, "seq", ahead)
    next_q = lax.ppermute(queries, "seq", behind)
    prev_v = lax.ppermute(values_in, "seq", ahead)
    next_c = lax.ppermute(cotangent, "seq", behind)
    sent = jnp.concatenate([queries, keys, values_in, cotangent], axis=1)
    sent, prev_k, next_q, prev_v, next_c = lax.optimization_barrier((sent, prev_k, next_q, prev_v, next_c))
    width = sent.shape[1]
    got = lax.all_to_all(sent.reshape(POS, OFF, width), "seq", 0, 0, tiled=True)
    got = got.reshape(STRIDE, width)

    row_nat, row_pack, row_o = call(
        row_fwd_kernel,
        [SMEM] + [heads()] * 6 + [heads(rows=8), whole(8, STRIDE)],
        [whole(24, STRIDE), whole(POS, 128), heads()],
        [shape(24, STRIDE), shape(POS, 128), shape(STRIDE, NH * HSZ, dtype=BF16)],
        [pltpu.VMEM((NH, 8, STRIDE), F32)],
        "row_fwd",
    )(bias, queries, prev_k, keys, prev_v, values_in, cotangent, w8, ret8)
    col_nat, stats = single(
        col_fwd_kernel, [shape(16, STRIDE), shape(POS, 2, 128)], name="col_fwd"
    )(got, w8, row_pack)
    stats = lax.all_to_all(stats, "seq", 0, 0, tiled=True)
    t, tc, part = single(
        merge_kernel, [shape(24, STRIDE), shape(16, STRIDE), shape(8, STRIDE)], name="merge"
    )(row_nat, col_nat, stats)
    next_t = lax.ppermute(t, "seq", behind)
    crit = doubling(part, "head", (1, 2))
    next_crit = lax.ppermute(crit, "seq", behind)

    back_width = 3 * NH * HSZ + HSZ
    col_out = single(
        col_bwd_kernel,
        shape(STRIDE, back_width, dtype=BF16),
        [pltpu.VMEM((QB, 2 * HSZ), F32), pltpu.VMEM((QB, HSZ), F32)],
        "col_bwd",
    )(got, w8, tc, t, crit, row_o)
    col_out, next_t, next_crit = lax.optimization_barrier((col_out, next_t, next_crit))
    back = lax.all_to_all(col_out.reshape(POS, OFF, back_width), "seq", 0, 0, tiled=True)
    back = back.reshape(STRIDE, back_width)

    row_out = call(
        row_bwd_kernel,
        [SMEM] + [heads()] * 8 + [heads(rows=8)] + [whole(24, STRIDE)] * 2 + [whole(8, STRIDE)] * 2,
        heads(width=3 * HSZ),
        shape(STRIDE, 3 * NH * HSZ),
        [
            pltpu.VMEM((2, STRIDE, HSZ), BF16),
            pltpu.VMEM((STRIDE, 2 * HSZ), F32),
            pltpu.VMEM((STRIDE, HSZ), F32),
        ],
        "row_bwd",
    )(
        bias, queries, next_q, prev_k, keys, prev_v, values_in, cotangent, next_c, w8, t, next_t, crit, next_crit
    )

    rows = 128
    grad = shape(STRIDE, NH * HSZ, dtype=BF16)
    by_rows = [pl.BlockSpec((rows, n), lambda i: (i, 0)) for n in (3 * NH * HSZ, back_width, NH * HSZ)]
    grad_q, grad_k, grad_v, grad_w = pl.pallas_call(
        final_kernel,
        grid=(STRIDE // rows,),
        in_specs=by_rows[0:2],
        out_specs=[by_rows[2]] * 3 + [whole(8, HSZ)],
        out_shape=[grad] * 3 + [shape(8, HSZ)],
        compiler_params=PARAMS,
        name="final_sum",
    )(row_out, back)
    return crit[0], grad_w[0:NH].reshape(NH * HSZ), grad_q, grad_k, grad_v


def solution(mesh):
    return jax.shard_map(
        body,
        mesh=mesh,
        in_specs=(
            P("seq", "head"),
            P("seq", "head"),
            P("seq", "head"),
            P("seq", "head"),
            P("head"),
            P("seq"),
        ),
        out_specs=(P("seq"), P("head"), P("seq", "head"), P("seq", "head"), P("seq", "head")),
        check_vma=False,
    )
```

```python
import functools

import jax
import jax.numpy as jnp
from jax import lax
from jax.experimental import pallas as pl
from jax.experimental.pallas import tpu as pltpu
from jax.sharding import PartitionSpec as P

HSZ = 128
STRIDE = 512
NH = 5
RUNS = ((0, 2), (2, 2), (4, 1))
POS = 64
OFF = 8
QB = 256
NEG = -1e30
SCALE = HSZ ** (-0.5)
VMEM = 60 * 1024 * 1024
SMALL_VMEM = 32 * 1024 * 1024
F32 = jnp.float32
BF16 = jnp.bfloat16


def iota(shape, dim):
    return lax.broadcasted_iota(jnp.int32, shape, dim)


def dot_nt(a, b):
    return lax.dot_general(a, b, (((1,), (1,)), ((), ())), preferred_element_type=F32)


def dot_nn(a, b):
    return lax.dot_general(a, b, (((1,), (0,)), ((), ())), preferred_element_type=F32)


def dot_tn(a, b):
    return lax.dot_general(a, b, (((0,), (0,)), ((), ())), preferred_element_type=F32)


def exact(a, b, dims):
    return lax.dot_general(
        a, b, (dims, ((), ())), preferred_element_type=F32, precision=lax.Precision.HIGHEST
    )


def pack(r):
    spread = (iota((16, 128), 1) // OFF == iota((16, 128), 0)).astype(F32)
    a = exact(r, spread, ((0,), (0,)))
    a = jnp.where(iota((512, 128), 0) % OFF == iota((512, 128), 1) % OFF, a, 0.0)
    gather = (iota((POS, 512), 1) // OFF == iota((POS, 512), 0)).astype(F32)
    return exact(gather, a, ((1,), (0,)))


def unpack(m):
    spread = (iota((512, POS), 0) // OFF == iota((512, POS), 1)).astype(F32)
    a = exact(spread, m, ((1,), (0,)))
    a = jnp.where(iota((512, 128), 0) % OFF == iota((512, 128), 1) % OFF, a, 0.0)
    gather = (iota((16, 128), 1) // OFF == iota((16, 128), 0)).astype(F32)
    return exact(gather, a, ((1,), (1,)))


def split3(x):
    hi = x.astype(BF16)
    rest = x - hi.astype(F32)
    mid = rest.astype(BF16)
    return hi, mid, (rest - mid.astype(F32)).astype(BF16)


def resid_columns(resid):
    hi, mid, lo = split3(resid)
    rows = jnp.concatenate([hi, mid, lo, jnp.zeros((13, 512), BF16)], axis=0)
    eye = (iota((16, 128), 0) == iota((16, 128), 1)).astype(BF16)
    return dot_tn(rows, eye).astype(BF16)


def col_masks():
    token, lane = iota((STRIDE, HSZ), 0), iota((STRIDE, HSZ), 1)
    off, pos = token % OFF, token // OFF
    is_off, is_pos = lane < OFF, (lane >= OFF) & (lane < OFF + POS)
    ka = (is_off & (lane == off)) | (is_pos & (lane - OFF == pos))
    qa = (is_off & (lane != off)) | (is_pos & (lane - OFF >= pos))
    return jnp.where(ka, 1.0, 0.0).astype(BF16), jnp.where(qa, -(2.0**100), 0.0).astype(BF16)


def col_scores(k, q, masks, qb):
    rows, at = slice(0, (qb + 1) * QB), slice(qb * QB, (qb + 1) * QB)
    kx = jnp.concatenate([k[rows], masks[0][rows]], axis=1)
    return dot_nt(kx, jnp.concatenate([q[at], masks[1][at]], axis=1))


def rsum(x):
    return jnp.sum(x, axis=0, keepdims=True)


def stats_of(s, dp, wv):
    top = jnp.max(s, axis=0, keepdims=True)
    e = jnp.exp((s - top) * SCALE)
    z = rsum(e)
    u = rsum(e * wv)
    c = rsum(e * dp)
    return top * SCALE + jnp.log(z), u / z, c / z, z, e


def wv_of(v, w):
    return jnp.sum(v.astype(F32) * w, axis=1, keepdims=True)


def row_window(kp_ref, k_ref, qb):
    runs = [kp_ref[0:QB, :], kp_ref[QB:, :], k_ref[0:QB, :], k_ref[QB:, :]]
    return jnp.concatenate(runs[qb : qb + 3], axis=0)


def upper():
    return iota((QB, QB), 0) > iota((QB, QB), 1)


def row_scores(kw, q, bias, qb):
    s = dot_nt(kw, q)
    up = upper()
    s0 = jnp.where(up, s[0:QB], NEG) + bias
    s1 = s[QB : 2 * QB]
    if qb == 0:
        s1 = s1 + bias
    s2 = jnp.where(up, NEG, s[2 * QB :])
    return jnp.concatenate([s0, s1, s2], axis=0)


def row_fwd_head(bias_ref, q_ref, kp_ref, k_ref, vp_ref, v_ref, c_ref, w_ref, st_ref, o_ref):
    w = w_ref[0:1, :]
    bias = bias_ref[0]
    for qb in range(2):
        at = slice(qb * QB, (qb + 1) * QB)
        kw = row_window(kp_ref, k_ref, qb)
        vw = row_window(vp_ref, v_ref, qb)
        s = row_scores(kw, q_ref[at, :], bias, qb)
        dp = dot_nt(vw, c_ref[at, :])
        lse, u, c, z, e = stats_of(s, dp, wv_of(vw, w))
        o_ref[:, at] = dot_tn(vw, e.astype(BF16)).astype(BF16)
        st_ref[:, at] = jnp.concatenate([lse, u, c, z, z, z, z, z], axis=0)


def row_fwd_kernel(*refs):
    *ins, o_ref, st_ref = refs
    row_fwd_head(*ins, st_ref, o_ref)


def row_fwd_last_kernel(*refs):
    *ins, ret_ref, col_ref = refs[: 9 + len(RUNS)]
    ins, done = ins[:8], ins[8:]
    o_ref, nat_ref, stats_ref, st_ref = refs[9 + len(RUNS) :]
    h = pl.program_id(0)
    row_fwd_head(*ins, st_ref.at[pl.ds(pl.multiple_of(8 * h, 8), 8)], o_ref)

    @pl.when(h == RUNS[-1][1] - 1)
    def _():
        rows = [[], [], [], []]
        for (_, n), ref in zip(RUNS, done + [st_ref]):
            for g in range(n):
                for i in range(4):
                    rows[i].append(ref[8 * g + i : 8 * g + i + 1, :])
        r = jnp.concatenate(rows[0] + rows[1] + rows[2] + [ret_ref[0:1, :]], axis=0)
        nat_ref[0:16, :] = r
        nat_ref[16:24, :] = jnp.concatenate(rows[3] + [jnp.zeros((3, STRIDE), F32)], axis=0)
        col = col_ref[...]
        stats_ref[:, 0, :] = pack(r)
        stats_ref[:, 1, :] = col
        stats_ref[:, 2, :] = jnp.concatenate([col[1:], jnp.zeros((1, 128), F32)], axis=0)
        stats_ref[:, 3, :] = jnp.zeros((POS, 128), F32)


def col_heads(got_ref, h):
    return (got_ref[:, (i * NH + h) * HSZ : (i * NH + h + 1) * HSZ] for i in range(4))


def col_fwd_kernel(got_ref, w_ref, nat_ref, out_ref):
    masks = col_masks()
    has = iota((1, STRIDE), 1) >= OFF
    rows = [[], [], []]
    for h in range(NH):
        q, k, v, c = col_heads(got_ref, h)
        wv = wv_of(v, w_ref[0:1, h * HSZ : (h + 1) * HSZ])
        parts = []
        for qb in range(2):
            s = col_scores(k, q, masks, qb)
            dp = dot_nt(v[0 : (qb + 1) * QB], c[qb * QB : (qb + 1) * QB])
            parts.append(stats_of(s, dp, wv[0 : (qb + 1) * QB])[0:3])
        for i in range(3):
            row = jnp.concatenate([parts[0][i], parts[1][i]], axis=1)
            rows[i].append(jnp.where(has, row, NEG if i == 0 else 0.0))
    r = jnp.concatenate(rows[0] + rows[1] + rows[2] + [jnp.zeros((1, STRIDE), F32)], axis=0)
    nat_ref[...] = r
    mine = pack(r)
    out_ref[...] = mine


def merge(r, c):
    lse_r, lse_c = r[0:5], c[0:5]
    top = jnp.maximum(lse_r, lse_c)
    lse = top + jnp.log(jnp.exp(lse_r - top) + jnp.exp(lse_c - top))
    a_r, a_c = jnp.exp(lse_r - lse), jnp.exp(lse_c - lse)
    u = a_r * r[5:10] + a_c * c[5:10]
    cc = a_r * r[10:15] + a_c * c[10:15]
    return jnp.concatenate([lse, u, cc, r[15:16]], axis=0), jnp.sum(u, axis=0, keepdims=True), a_r


def merge_kernel(got_ref, rnat_ref, rnext_ref, cnat_ref, t_ref, tc_ref, tn_ref, part_ref):
    nat = rnat_ref[...]
    t, part, a_r = merge(nat[0:16], unpack(got_ref[:, 1, :]))
    t_ref[0:16, :] = t
    t_ref[16:21, :] = a_r / nat[16:21]
    t_ref[21:24, :] = jnp.zeros((3, STRIDE), F32)
    tc_ref[...], partc, _ = merge(unpack(got_ref[:, 0, :]), cnat_ref[...])
    tn_ref[...], partn, _ = merge(rnext_ref[0:16, :], unpack(got_ref[:, 2, :]))
    part_ref[...] = jnp.concatenate([part, partc, partn, jnp.zeros((5, STRIDE), F32)], axis=0)


def resid_of(t_ref, crit, role):
    return crit[role : role + 1] - t_ref[15:16, :]


def bwd_lanes(t_ref, resid, h):
    lse = t_ref[pl.ds(h, 1), :]
    u = t_ref[pl.ds(NH + h, 1), :]
    c = t_ref[pl.ds(2 * NH + h, 1), :]
    return lse, c + resid * u


def grads(s, dp, wv, lse, resid, dsum):
    p = jnp.exp(s * SCALE - lse)
    g = p * (dp + (wv * resid - dsum))
    return p.astype(BF16), g.astype(BF16)


def col_bwd_kernel(
    got_ref, w_ref, tc_ref, t_ref, p0_ref, p1_ref, p2_ref, p3_ref, *refs
):
    o_refs, (hbm_ref, crit_ref, out_ref, dv_ref, dk_ref, held_ref, sems) = refs[: len(RUNS)], refs[len(RUNS) :]
    fetch = [
        pltpu.make_async_copy(ref, held_ref.at[at * HSZ : (at + n) * HSZ], sems.at[NH + 1 + i])
        for i, ((at, n), ref) in enumerate(zip(RUNS, o_refs))
    ]
    for copy in fetch:
        copy.start()

    def send(i, width):
        at = slice(i * 3 * HSZ, i * 3 * HSZ + width)
        copy = pltpu.make_async_copy(out_ref.at[:, at], hbm_ref.at[:, at], sems.at[i])
        copy.start()
        return copy

    copies = []
    masks = col_masks()
    crit = (p0_ref[...] + p1_ref[...]) + (p2_ref[...] + p3_ref[...])
    crit_ref[...] = crit
    resid = resid_of(tc_ref, crit, 1)
    rc = resid_columns(resid)
    resid_r = resid_of(t_ref, crit, 0)
    gws = []
    for h in range(NH):
        q, k, v, c = col_heads(got_ref, h)
        w = w_ref[0:1, h * HSZ : (h + 1) * HSZ]
        wv = wv_of(v, w)
        lse, dsum = bwd_lanes(tc_ref, resid, h)
        at_q, at_k, at_v = (slice((3 * h + i) * HSZ, (3 * h + i + 1) * HSZ) for i in range(3))
        for qb in range(2):
            at = slice(qb * QB, (qb + 1) * QB)
            rows = (qb + 1) * QB
            s = col_scores(k, q, masks, qb)
            dp = dot_nt(v[0:rows], c[at])
            p, g = grads(s, dp, wv[0:rows], lse[:, at], resid[:, at], dsum[:, at])
            dv = dot_nn(p, jnp.concatenate([c[at], rc[at]], axis=1))
            dk = dot_nn(g, q[at])
            out_ref[at, at_q] = (dot_tn(g, k[0:rows]) * SCALE).astype(BF16)
            if qb == 0:
                dv_ref[...] = dv
                dk_ref[...] = dk
            else:
                dv = jnp.concatenate([dv[0:QB] + dv_ref[...], dv[QB:]], axis=0)
                dk = jnp.concatenate([dk[0:QB] + dk_ref[...], dk[QB:]], axis=0)
        cj = jnp.sum(dv[:, HSZ:], axis=1, keepdims=True)
        out_ref[:, at_k] = (dk * SCALE).astype(BF16)
        out_ref[:, at_v] = (dv[:, 0:HSZ] + cj * w).astype(BF16)
        gw = rsum(cj * v.astype(F32))
        gws.append(gw)
        copies.append(send(h, 3 * HSZ))
    for copy in fetch:
        copy.wait()
    for h in range(NH):
        weight = resid_r * t_ref[16 + h : 17 + h, :]
        weight = jnp.concatenate(split3(weight) + (jnp.zeros((13, STRIDE), BF16),), axis=0)
        gws[h] = gws[h] + rsum(dot_nt(weight, held_ref[h * HSZ : (h + 1) * HSZ]))
    tile = jnp.concatenate(gws + [jnp.zeros((3, HSZ), F32)], axis=0)
    tile = jnp.broadcast_to(tile[None], (POS, OFF, HSZ)).reshape(STRIDE, HSZ)
    out_ref[:, 3 * NH * HSZ :] = tile.astype(BF16)
    copies.append(send(NH, HSZ))
    for copy in copies:
        copy.wait()


def row_bwd_kernel(
    bias_ref, q_ref, qn_ref, kp_ref, k_ref, vp_ref, v_ref, c_ref, cn_ref, w_ref, t_ref, tn_ref, crit_ref,
    out_ref, rc_ref, dv_ref, dk_ref, *, start,
):
    step = pl.program_id(0)
    h = start + step
    resid = resid_of(t_ref, crit_ref[...], 0)
    resid_n = resid_of(tn_ref, crit_ref[...], 2)

    @pl.when(step == 0)
    def _():
        rc_ref[0] = resid_columns(resid)
        rc_ref[1] = resid_columns(resid_n)

    lse, dsum = bwd_lanes(t_ref, resid, h)
    lse_n, dsum_n = bwd_lanes(tn_ref, resid_n, h)
    w = w_ref[0:1, :]
    wv = wv_of(v_ref[...], w)
    wvp = wv_of(vp_ref[...], w)
    wvx = jnp.concatenate([wvp, wv], axis=0)
    for qb in range(2):
        at = slice(qb * QB, (qb + 1) * QB)
        kw = row_window(kp_ref, k_ref, qb)
        vw = row_window(vp_ref, v_ref, qb)
        s = row_scores(kw, q_ref[at, :], bias_ref[0], qb)
        dp = dot_nt(vw, c_ref[at, :])
        p, g = grads(s, dp, wvx[qb * QB : (qb + 3) * QB], lse[:, at], resid[:, at], dsum[:, at])
        out_ref[at, 0:HSZ] = dot_tn(g, kw) * SCALE
        own = (2 - qb) * QB
        caug = jnp.concatenate([c_ref[at, :], rc_ref[0, at, :]], axis=1)
        dv = dot_nn(p[own:], caug)
        dk = dot_nn(g[own:], q_ref[at, :])
        if qb == 0:
            dv_ref[0:QB, :] = dv
            dk_ref[0:QB, :] = dk
        else:
            dv_ref[0:QB, :] += dv[0:QB]
            dk_ref[0:QB, :] += dk[0:QB]
            dv_ref[QB:, :] = dv[QB:]
            dk_ref[QB:, :] = dk[QB:]
    up = upper()
    for qb in range(2):
        at = slice(qb * QB, (qb + 1) * QB)
        kw, vw = k_ref[qb * QB :, :], v_ref[qb * QB :, :]
        s = dot_nt(kw, qn_ref[at, :]) + bias_ref[1]
        s0 = jnp.where(up, s[0:QB], NEG)
        s = jnp.concatenate([s0, s[QB:]], axis=0) if qb == 0 else s0
        dp = dot_nt(vw, cn_ref[at, :])
        p, g = grads(s, dp, wv[qb * QB :], lse_n[:, at], resid_n[:, at], dsum_n[:, at])
        caug = jnp.concatenate([cn_ref[at, :], rc_ref[1, at, :]], axis=1)
        dv_ref[qb * QB :, :] += dot_nn(p, caug)
        dk_ref[qb * QB :, :] += dot_nn(g, qn_ref[at, :])
    cj = jnp.sum(dv_ref[:, HSZ:], axis=1, keepdims=True)
    out_ref[:, HSZ : 2 * HSZ] = dk_ref[...] * SCALE
    out_ref[:, 2 * HSZ :] = dv_ref[:, 0:HSZ] + cj * w


def final_kernel(*refs):
    row_refs, (col_ref, q_ref, k_ref, v_ref, gw_ref) = refs[: len(RUNS)], refs[len(RUNS) :]
    step, rows = pl.program_id(0), q_ref.shape[0]
    col = col_ref[pl.ds(pl.multiple_of(step * rows, rows), rows), :]
    for (start, n), row_ref in zip(RUNS, row_refs):
        for h in range(start, start + n):
            for i, ref in enumerate((q_ref, k_ref, v_ref)):
                at, near = (3 * h + i) * HSZ, (3 * (h - start) + i) * HSZ
                x = row_ref[:, near : near + HSZ] + col[:, at : at + HSZ].astype(F32)
                ref[:, h * HSZ : (h + 1) * HSZ] = x.astype(BF16)
    tiles = col[:, 3 * NH * HSZ :].astype(F32)
    tile = jnp.sum(tiles.reshape(rows // OFF, OFF, HSZ), axis=0)

    @pl.when(step == 0)
    def _():
        gw_ref[...] = tile

    @pl.when(step > 0)
    def _():
        gw_ref[...] += tile


def heads(at=0, rows=STRIDE, width=HSZ):
    return pl.BlockSpec((rows, width), lambda h: (0, at + h))


def whole(*shape):
    return pl.BlockSpec(shape, lambda h: (0,) * len(shape))


SMEM = pl.BlockSpec(memory_space=pltpu.SMEM)
PARAMS = pltpu.CompilerParams(vmem_limit_bytes=VMEM, dimension_semantics=("arbitrary",))


def shape(*dims, dtype=F32):
    return jax.ShapeDtypeStruct(dims, dtype)


def hbm(*dims, dtype=F32):
    return pltpu.HBM(dims, dtype)


def cost(us):
    return pl.CostEstimate(flops=int(us * 1e9), bytes_accessed=0, transcendentals=0)


def call(kernel, steps, ins, outs, out_shape, scratch=(), name=None, us=1):
    return pl.pallas_call(
        kernel,
        cost_estimate=cost(us),
        grid=(steps,),
        in_specs=ins,
        out_specs=outs,
        out_shape=out_shape,
        scratch_shapes=list(scratch),
        compiler_params=PARAMS,
        name=name,
    )


def in_hbm(x):
    return pltpu.with_memory_space_constraint(x, pltpu.HBM)


def single(kernel, held, args, out_shape, scratch=(), name=None, out_specs=None, far=(), us=1):
    vmem = pl.BlockSpec(memory_space=pltpu.VMEM)
    return pl.pallas_call(
        kernel,
        cost_estimate=cost(us),
        in_specs=[vmem] * (len(held) + len(args)) + [pl.BlockSpec(memory_space=pltpu.HBM)] * len(far),
        out_specs=jax.tree.map(lambda _: vmem, out_shape) if out_specs is None else out_specs,
        out_shape=out_shape,
        scratch_shapes=list(scratch),
        compiler_params=pltpu.CompilerParams(vmem_limit_bytes=SMALL_VMEM),
        name=name,
    )(*[pltpu.with_memory_space_constraint(x, pltpu.VMEM) for x in held], *args, *[in_hbm(x) for x in far])


def exchange(*arrays):
    x = jnp.concatenate(arrays, axis=1)
    x = lax.all_to_all(x.reshape(POS, OFF, x.shape[1]), "seq", 0, 0, tiled=True)
    return x.reshape(STRIDE, x.shape[2])


def body(queries, keys, values_in, cotangent, w_value, returns):
    seq = lax.axis_size("seq")
    at = lax.axis_index("seq")
    bias = jnp.where(jnp.stack([at == 0, at == seq - 1]), NEG, 0.0).astype(F32)
    w8 = jnp.broadcast_to(w_value[None, :], (8, w_value.shape[0]))
    ret8 = jnp.broadcast_to(returns[None, :], (8, STRIDE))

    got = exchange(queries, keys, values_in, cotangent)
    ahead = [(i, i + 1) for i in range(seq - 1)]
    behind = [(i + 1, i) for i in range(seq - 1)]
    def run(x, start, n):
        return x[:, start * HSZ : (start + n) * HSZ]

    prev = [
        lax.ppermute(jnp.concatenate([run(keys, *r), run(values_in, *r)], axis=1), "seq", ahead) for r in RUNS
    ]
    after = [lax.ppermute(x, "seq", behind) for x in (queries, cotangent)]
    col_nat, col_pack = single(
        col_fwd_kernel, (got,), (w8,), [hbm(16, STRIDE), hbm(POS, 128)], name="col_fwd", us=4
    )
    w8, col_nat, col_pack = lax.optimization_barrier((w8, col_nat, col_pack))

    done, row_o = [], []
    for (start, n), kv in zip(RUNS, prev):
        there = heads(start)
        ins = [SMEM, there, heads(), there, heads(n), there, there, heads(start, rows=8)]
        args = [bias, queries, kv, keys, kv, values_in, cotangent, w8]
        out_specs = [pl.BlockSpec((HSZ, STRIDE), lambda h: (h, 0))]
        out_shape = [shape(n * HSZ, STRIDE, dtype=BF16)]
        if start + n < NH:
            out_specs.append(pl.BlockSpec((8, STRIDE), lambda h: (h, 0)))
            out_shape.append(shape(8 * n, STRIDE))
            o, st = call(row_fwd_kernel, n, ins, out_specs, out_shape, name="row_fwd", us=2 * n)(*args)
            done.append(st)
        else:
            ins += [whole(8 * m, STRIDE) for _, m in RUNS[:-1]] + [whole(8, STRIDE), whole(POS, 128)]
            out_specs += [whole(24, STRIDE), whole(POS, 4, 128)]
            out_shape += [shape(24, STRIDE), shape(POS, 4, 128)]
            scratch = [pltpu.VMEM((8 * n, STRIDE), F32)]
            o, row_nat, stats = call(
                row_fwd_last_kernel, n, ins, out_specs, out_shape, scratch, "row_fwd_last", 2 * n + 1
            )(*args, *done, ret8, col_pack)
        row_o.append(o)
    next_nat = lax.ppermute(row_nat, "seq", behind)
    stats, next_q, next_c = lax.optimization_barrier((stats, *after))
    stats = lax.all_to_all(stats, "seq", 0, 0, tiled=True)
    t, tc, tn, part = single(
        merge_kernel,
        (stats,),
        (row_nat, next_nat, col_nat),
        [shape(24, STRIDE), shape(16, STRIDE), hbm(16, STRIDE), shape(8, STRIDE)],
        name="merge",
    )
    size = lax.axis_size("head")
    parts = [part] + [lax.ppermute(part, "head", [(i, i ^ d) for i in range(size)]) for d in (1, 2, 3)]

    back_width = 3 * NH * HSZ + HSZ
    col_out, crit = single(
        col_bwd_kernel,
        (got,),
        (w8, tc, t, *parts),
        [hbm(STRIDE, back_width, dtype=BF16), hbm(8, STRIDE)],
        [
            pltpu.VMEM((STRIDE, back_width), BF16),
            pltpu.VMEM((QB, 2 * HSZ), F32),
            pltpu.VMEM((QB, HSZ), F32),
            pltpu.VMEM((NH * HSZ, STRIDE), BF16),
            pltpu.SemaphoreType.DMA((NH + 1 + len(RUNS),)),
        ],
        "col_bwd",
        [pl.BlockSpec(memory_space=pltpu.HBM), pl.BlockSpec(memory_space=pltpu.VMEM)],
        row_o,
    )
    back = lax.all_to_all(col_out.reshape(POS, OFF, back_width), "seq", 0, 0, tiled=True)
    back = back.reshape(STRIDE, back_width)

    row_out = []
    for (start, steps), kv in zip(RUNS, prev):
        there = heads(start)
        row_out.append(
            call(
                functools.partial(row_bwd_kernel, start=start),
                steps,
                [SMEM, there, there, heads(), there, heads(steps), there, there, there, heads(start, rows=8)]
                + [whole(24, STRIDE), whole(16, STRIDE), whole(8, STRIDE)],
                heads(width=3 * HSZ),
                shape(STRIDE, 3 * steps * HSZ),
                [
                    pltpu.VMEM((2, STRIDE, HSZ), BF16),
                    pltpu.VMEM((STRIDE, 2 * HSZ), F32),
                    pltpu.VMEM((STRIDE, HSZ), F32),
                ],
                "row_bwd",
                3 * steps,
            )(bias, queries, next_q, kv, keys, kv, values_in, cotangent, next_c, w8, t, tn, crit)
        )

    grad = shape(STRIDE, NH * HSZ, dtype=BF16)
    rows = STRIDE // 4
    by_rows = [pl.BlockSpec((rows, n), lambda i: (i, 0)) for n in [3 * n * HSZ for _, n in RUNS] + [NH * HSZ]]
    grad_q, grad_k, grad_v, grad_w = pl.pallas_call(
        final_kernel,
        grid=(STRIDE // rows,),
        in_specs=by_rows[:-1] + [pl.BlockSpec(memory_space=pltpu.VMEM)],
        out_specs=[by_rows[-1]] * 3 + [whole(8, HSZ)],
        out_shape=[grad] * 3 + [shape(8, HSZ)],
        compiler_params=pltpu.CompilerParams(vmem_limit_bytes=SMALL_VMEM, dimension_semantics=("arbitrary",)),
        name="final_sum",
    )(*[in_hbm(x) for x in row_out], pltpu.with_memory_space_constraint(back, pltpu.VMEM))
    return crit[0], grad_w[0:NH].reshape(NH * HSZ), grad_q, grad_k, grad_v


def solution(mesh):
    return jax.shard_map(
        body,
        mesh=mesh,
        in_specs=(
            P("seq", "head"),
            P("seq", "head"),
            P("seq", "head"),
            P("seq", "head"),
            P("head"),
            P("seq"),
        ),
        out_specs=(P("seq"), P("head"), P("seq", "head"), P("seq", "head"), P("seq", "head")),
        check_vma=False,
    )
```

```python
import functools

import jax
import jax.numpy as jnp
from jax import lax
from jax.experimental import pallas as pl
from jax.experimental.pallas import tpu as pltpu
from jax.sharding import PartitionSpec as P

HSZ = 128
STRIDE = 512
NH = 5
RUNS = ((0, 2), (2, 2), (4, 1))
O_RUNS = ((0, 5),) + tuple((NH + at, n) for at, n in RUNS)
POS = 64
OFF = 8
QB = 256
NEG = -1e30
SCALE = HSZ ** (-0.5)
VMEM = 60 * 1024 * 1024
SMALL_VMEM = 32 * 1024 * 1024
F32 = jnp.float32
BF16 = jnp.bfloat16


def iota(shape, dim):
    return lax.broadcasted_iota(jnp.int32, shape, dim)


def dot_nt(a, b):
    return lax.dot_general(a, b, (((1,), (1,)), ((), ())), preferred_element_type=F32)


def dot_nn(a, b):
    return lax.dot_general(a, b, (((1,), (0,)), ((), ())), preferred_element_type=F32)


def dot_tn(a, b):
    return lax.dot_general(a, b, (((0,), (0,)), ((), ())), preferred_element_type=F32)


def exact(a, b, dims):
    return lax.dot_general(
        a, b, (dims, ((), ())), preferred_element_type=F32, precision=lax.Precision.HIGHEST
    )


def pack(r):
    spread = (iota((16, 128), 1) // OFF == iota((16, 128), 0)).astype(F32)
    a = exact(r, spread, ((0,), (0,)))
    a = jnp.where(iota((512, 128), 0) % OFF == iota((512, 128), 1) % OFF, a, 0.0)
    gather = (iota((POS, 512), 1) // OFF == iota((POS, 512), 0)).astype(F32)
    return exact(gather, a, ((1,), (0,)))


def unpack(m):
    spread = (iota((512, POS), 0) // OFF == iota((512, POS), 1)).astype(F32)
    a = exact(spread, m, ((1,), (0,)))
    a = jnp.where(iota((512, 128), 0) % OFF == iota((512, 128), 1) % OFF, a, 0.0)
    gather = (iota((16, 128), 1) // OFF == iota((16, 128), 0)).astype(F32)
    return exact(gather, a, ((1,), (1,)))


def split3(x):
    hi = x.astype(BF16)
    rest = x - hi.astype(F32)
    mid = rest.astype(BF16)
    return hi, mid, (rest - mid.astype(F32)).astype(BF16)


def resid_columns(resid):
    hi, mid, lo = split3(resid)
    rows = jnp.concatenate([hi, mid, lo, jnp.zeros((13, 512), BF16)], axis=0)
    eye = (iota((16, 128), 0) == iota((16, 128), 1)).astype(BF16)
    return dot_tn(rows, eye).astype(BF16)


def col_masks():
    token, lane = iota((STRIDE, HSZ), 0), iota((STRIDE, HSZ), 1)
    off, pos = token % OFF, token // OFF
    is_off, is_pos = lane < OFF, (lane >= OFF) & (lane < OFF + POS)
    ka = (is_off & (lane == off)) | (is_pos & (lane - OFF == pos))
    qa = (is_off & (lane != off)) | (is_pos & (lane - OFF >= pos))
    return jnp.where(ka, 1.0, 0.0).astype(BF16), jnp.where(qa, -(2.0**100), 0.0).astype(BF16)


def col_scores(k, q, masks, qb):
    rows, at = slice(0, (qb + 1) * QB), slice(qb * QB, (qb + 1) * QB)
    kx = jnp.concatenate([k[rows], masks[0][rows]], axis=1)
    return dot_nt(kx, jnp.concatenate([q[at], masks[1][at]], axis=1))


def rsum(x):
    return jnp.sum(x, axis=0, keepdims=True)


def stats_of(s, dp, wv):
    top = jnp.max(s, axis=0, keepdims=True)
    e = jnp.exp((s - top) * SCALE)
    z = rsum(e)
    u = rsum(e * wv)
    c = rsum(e * dp)
    m = top * SCALE
    return m + jnp.log(z), u / z, c / z, m, e


def wv_of(v, w):
    return jnp.sum(v.astype(F32) * w, axis=1, keepdims=True)


def row_window(kp_ref, k_ref, qb):
    runs = [kp_ref[0:QB, :], kp_ref[QB:, :], k_ref[0:QB, :], k_ref[QB:, :]]
    return jnp.concatenate(runs[qb : qb + 3], axis=0)


def upper():
    return iota((QB, QB), 0) > iota((QB, QB), 1)


def row_scores(kw, q, bias, qb):
    s = dot_nt(kw, q)
    up = upper()
    s0 = jnp.where(up, s[0:QB], NEG) + bias
    s1 = s[QB : 2 * QB]
    if qb == 0:
        s1 = s1 + bias
    s2 = jnp.where(up, NEG, s[2 * QB :])
    return jnp.concatenate([s0, s1, s2], axis=0)


def put_stats(at, s, dp, v, w, st_ref, o_ref):
    lse, u, c, m, e = stats_of(s, dp, wv_of(v, w))
    o_ref[:, at] = dot_tn(v, e.astype(BF16)).astype(BF16)
    st_ref[:, at] = jnp.concatenate([lse, u, c, m, m, m, m, m], axis=0)


def row_own_kernel(q_ref, k_ref, v_ref, c_ref, w_ref, o_ref, st_ref):
    for qb in range(2):
        at, rows = slice(qb * QB, (qb + 1) * QB), (qb + 1) * QB
        s = dot_nt(k_ref[0:rows, :], q_ref[at, :])
        last = jnp.where(upper(), NEG, s[qb * QB :])
        s = jnp.concatenate([s[0:QB], last], axis=0) if qb else last
        put_stats(at, s, dot_nt(v_ref[0:rows, :], c_ref[at, :]), v_ref[0:rows, :], w_ref[0:1, :], st_ref, o_ref)


def cross_scores(k_ref, qn_ref, bias, qb):
    s = dot_nt(k_ref[qb * QB :, :], qn_ref[qb * QB : (qb + 1) * QB, :]) + bias
    first = jnp.where(upper(), s[0:QB], NEG)
    return first if qb else jnp.concatenate([first, s[QB:]], axis=0)


def row_cross_kernel(bias_ref, q_ref, k_ref, v_ref, c_ref, w_ref, o_ref, st_ref):
    for qb in range(2):
        at = slice(qb * QB, (qb + 1) * QB)
        s = cross_scores(k_ref, q_ref, bias_ref[0], qb)
        v = v_ref[qb * QB :, :]
        put_stats(at, s, dot_nt(v, c_ref[at, :]), v, w_ref[0:1, :], st_ref, o_ref)


def log_add(x, y):
    top = jnp.maximum(x, y)
    return top + jnp.log(jnp.exp(x - top) + jnp.exp(y - top))


def row_last_kernel(*refs):
    *ins, own_ref, ret_ref, col_ref = refs[: 8 + len(RUNS)]
    ins, done = ins[:6], ins[6:]
    o_ref, nat_ref, stats_ref, st_ref = refs[8 + len(RUNS) :]
    h = pl.program_id(0)
    row_cross_kernel(*ins, o_ref, st_ref.at[pl.ds(pl.multiple_of(8 * h, 8), 8)])

    @pl.when(h == RUNS[-1][1] - 1)
    def _():
        cross = [ref[8 * g : 8 * g + 8, :] for (_, n), ref in zip(RUNS, done + [st_ref]) for g in range(n)]
        own = [own_ref[8 * g : 8 * g + 8, :] for g in range(NH)]

        def rows(parts, i):
            return jnp.concatenate([x[i : i + 1] for x in parts], axis=0)

        lse_o, lse_p = rows(own, 0), rows(cross, 0)
        lse = log_add(lse_o, lse_p)
        a_o, a_p = jnp.exp(lse_o - lse), jnp.exp(lse_p - lse)
        u, c = (a_o * rows(own, i) + a_p * rows(cross, i) for i in (1, 2))
        r = jnp.concatenate([lse, u, c, ret_ref[0:1, :]], axis=0)
        nat_ref[0:16, :] = r
        nat_ref[16:32, :] = jnp.concatenate([rows(own, 3), rows(cross, 3), jnp.zeros((6, STRIDE), F32)], axis=0)
        col = col_ref[...]
        stats_ref[:, 0, :] = pack(r)
        stats_ref[:, 1, :] = col
        stats_ref[:, 2, :] = jnp.concatenate([col[1:], jnp.zeros((1, 128), F32)], axis=0)
        stats_ref[:, 3, :] = jnp.zeros((POS, 128), F32)


def col_heads(got_ref, h):
    return (got_ref[:, (i * NH + h) * HSZ : (i * NH + h + 1) * HSZ] for i in range(4))


def col_fwd_kernel(got_ref, w_ref, nat_ref, out_ref):
    masks = col_masks()
    has = iota((1, STRIDE), 1) >= OFF
    rows = [[], [], []]
    for h in range(NH):
        q, k, v, c = col_heads(got_ref, h)
        wv = wv_of(v, w_ref[0:1, h * HSZ : (h + 1) * HSZ])
        parts = []
        for qb in range(2):
            s = col_scores(k, q, masks, qb)
            dp = dot_nt(v[0 : (qb + 1) * QB], c[qb * QB : (qb + 1) * QB])
            parts.append(stats_of(s, dp, wv[0 : (qb + 1) * QB])[0:3])
        for i in range(3):
            row = jnp.concatenate([parts[0][i], parts[1][i]], axis=1)
            rows[i].append(jnp.where(has, row, NEG if i == 0 else 0.0))
    r = jnp.concatenate(rows[0] + rows[1] + rows[2] + [jnp.zeros((1, STRIDE), F32)], axis=0)
    nat_ref[...] = r
    mine = pack(r)
    out_ref[...] = mine


def merge(r, c):
    lse_r, lse_c = r[0:5], c[0:5]
    lse = log_add(lse_r, lse_c)
    a_r, a_c = jnp.exp(lse_r - lse), jnp.exp(lse_c - lse)
    u = a_r * r[5:10] + a_c * c[5:10]
    cc = a_r * r[10:15] + a_c * c[10:15]
    return jnp.concatenate([lse, u, cc, r[15:16]], axis=0), jnp.sum(u, axis=0, keepdims=True)


def merge_kernel(got_ref, rnat_ref, rnext_ref, cnat_ref, t_ref, tc_ref, tn_ref, part_ref):
    nat = rnat_ref[...]
    t, part = merge(nat[0:16], unpack(got_ref[:, 1, :]))
    weight = jnp.exp(nat[16 : 16 + 2 * NH] - jnp.concatenate([t[0:NH], t[0:NH]], axis=0))
    t_ref[0:16, :] = t
    t_ref[16:32, :] = jnp.concatenate([weight, jnp.zeros((16 - 2 * NH, STRIDE), F32)], axis=0)
    tc_ref[...], partc = merge(unpack(got_ref[:, 0, :]), cnat_ref[...])
    tn_ref[...], partn = merge(rnext_ref[0:16, :], unpack(got_ref[:, 2, :]))
    part_ref[...] = jnp.concatenate([part, partc, partn, jnp.zeros((5, STRIDE), F32)], axis=0)


def resid_of(t_ref, crit, role):
    return crit[role : role + 1] - t_ref[15:16, :]


def bwd_lanes(t_ref, resid, h):
    lse = t_ref[pl.ds(h, 1), :]
    u = t_ref[pl.ds(NH + h, 1), :]
    c = t_ref[pl.ds(2 * NH + h, 1), :]
    return lse, c + resid * u


def grads(s, dp, wv, lse, resid, dsum):
    p = jnp.exp(s * SCALE - lse)
    g = p * (dp + (wv * resid - dsum))
    return p.astype(BF16), g.astype(BF16)


def col_bwd_kernel(
    got_ref, w_ref, tc_ref, t_ref, p0_ref, p1_ref, p2_ref, p3_ref, *refs
):
    *o_refs, hbm_ref, crit_ref, out_ref, dv_ref, dk_ref, held_ref, sems = refs
    fetch = [
        pltpu.make_async_copy(ref, held_ref.at[at * HSZ : (at + n) * HSZ], sems.at[NH + 1 + i])
        for i, ((at, n), ref) in enumerate(zip(O_RUNS, o_refs))
    ]
    for copy in fetch:
        copy.start()

    def send(i, width):
        at = slice(i * 3 * HSZ, i * 3 * HSZ + width)
        copy = pltpu.make_async_copy(out_ref.at[:, at], hbm_ref.at[:, at], sems.at[i])
        copy.start()
        return copy

    copies = []
    masks = col_masks()
    crit = (p0_ref[...] + p1_ref[...]) + (p2_ref[...] + p3_ref[...])
    crit_ref[...] = crit
    resid = resid_of(tc_ref, crit, 1)
    rc = resid_columns(resid)
    resid_r = resid_of(t_ref, crit, 0)
    gws = []
    for h in range(NH):
        q, k, v, c = col_heads(got_ref, h)
        w = w_ref[0:1, h * HSZ : (h + 1) * HSZ]
        wv = wv_of(v, w)
        lse, dsum = bwd_lanes(tc_ref, resid, h)
        at_q, at_k, at_v = (slice((3 * h + i) * HSZ, (3 * h + i + 1) * HSZ) for i in range(3))
        for qb in range(2):
            at = slice(qb * QB, (qb + 1) * QB)
            rows = (qb + 1) * QB
            s = col_scores(k, q, masks, qb)
            dp = dot_nt(v[0:rows], c[at])
            p, g = grads(s, dp, wv[0:rows], lse[:, at], resid[:, at], dsum[:, at])
            dv = dot_nn(p, jnp.concatenate([c[at], rc[at]], axis=1))
            dk = dot_nn(g, q[at])
            out_ref[at, at_q] = (dot_tn(g, k[0:rows]) * SCALE).astype(BF16)
            if qb == 0:
                dv_ref[...] = dv
                dk_ref[...] = dk
            else:
                dv = jnp.concatenate([dv[0:QB] + dv_ref[...], dv[QB:]], axis=0)
                dk = jnp.concatenate([dk[0:QB] + dk_ref[...], dk[QB:]], axis=0)
        cj = jnp.sum(dv[:, HSZ:], axis=1, keepdims=True)
        out_ref[:, at_k] = (dk * SCALE).astype(BF16)
        out_ref[:, at_v] = (dv[:, 0:HSZ] + cj * w).astype(BF16)
        gw = rsum(cj * v.astype(F32))
        gws.append(gw)
        copies.append(send(h, 3 * HSZ))
    for copy in fetch:
        copy.wait()
    for h in range(2 * NH):
        weight = resid_r * t_ref[16 + h : 17 + h, :]
        weight = jnp.concatenate(split3(weight) + (jnp.zeros((13, STRIDE), BF16),), axis=0)
        gws[h % NH] = gws[h % NH] + rsum(dot_nt(weight, held_ref[h * HSZ : (h + 1) * HSZ]))
    tile = jnp.concatenate(gws + [jnp.zeros((3, HSZ), F32)], axis=0)
    tile = jnp.broadcast_to(tile[None], (POS, OFF, HSZ)).reshape(STRIDE, HSZ)
    out_ref[:, 3 * NH * HSZ :] = tile.astype(BF16)
    copies.append(send(NH, HSZ))
    for copy in copies:
        copy.wait()


def row_bwd_kernel(
    bias_ref, q_ref, qn_ref, kp_ref, k_ref, vp_ref, v_ref, c_ref, cn_ref, w_ref, t_ref, tn_ref, crit_ref,
    out_ref, rc_ref, dv_ref, dk_ref, *, start,
):
    step = pl.program_id(0)
    h = start + step
    resid = resid_of(t_ref, crit_ref[...], 0)
    resid_n = resid_of(tn_ref, crit_ref[...], 2)

    @pl.when(step == 0)
    def _():
        rc_ref[0] = resid_columns(resid)
        rc_ref[1] = resid_columns(resid_n)

    lse, dsum = bwd_lanes(t_ref, resid, h)
    lse_n, dsum_n = bwd_lanes(tn_ref, resid_n, h)
    w = w_ref[0:1, :]
    wv = wv_of(v_ref[...], w)
    wvp = wv_of(vp_ref[...], w)
    wvx = jnp.concatenate([wvp, wv], axis=0)
    for qb in range(2):
        at = slice(qb * QB, (qb + 1) * QB)
        kw = row_window(kp_ref, k_ref, qb)
        vw = row_window(vp_ref, v_ref, qb)
        s = row_scores(kw, q_ref[at, :], bias_ref[0], qb)
        dp = dot_nt(vw, c_ref[at, :])
        p, g = grads(s, dp, wvx[qb * QB : (qb + 3) * QB], lse[:, at], resid[:, at], dsum[:, at])
        out_ref[at, 0:HSZ] = dot_tn(g, kw) * SCALE
        own = (2 - qb) * QB
        caug = jnp.concatenate([c_ref[at, :], rc_ref[0, at, :]], axis=1)
        dv = dot_nn(p[own:], caug)
        dk = dot_nn(g[own:], q_ref[at, :])
        if qb == 0:
            dv_ref[0:QB, :] = dv
            dk_ref[0:QB, :] = dk
        else:
            dv_ref[0:QB, :] += dv[0:QB]
            dk_ref[0:QB, :] += dk[0:QB]
            dv_ref[QB:, :] = dv[QB:]
            dk_ref[QB:, :] = dk[QB:]
    for qb in range(2):
        at = slice(qb * QB, (qb + 1) * QB)
        vw = v_ref[qb * QB :, :]
        s = cross_scores(k_ref, qn_ref, bias_ref[1], qb)
        dp = dot_nt(vw, cn_ref[at, :])
        p, g = grads(s, dp, wv[qb * QB :], lse_n[:, at], resid_n[:, at], dsum_n[:, at])
        caug = jnp.concatenate([cn_ref[at, :], rc_ref[1, at, :]], axis=1)
        dv_ref[qb * QB :, :] += dot_nn(p, caug)
        dk_ref[qb * QB :, :] += dot_nn(g, qn_ref[at, :])
    cj = jnp.sum(dv_ref[:, HSZ:], axis=1, keepdims=True)
    out_ref[:, HSZ : 2 * HSZ] = dk_ref[...] * SCALE
    out_ref[:, 2 * HSZ :] = dv_ref[:, 0:HSZ] + cj * w


def final_kernel(col_ref, *refs):
    n = len(RUNS)
    row_refs, out_refs, gw_ref, refs = refs[:n], refs[n : n + 3], refs[n + 3], refs[n + 4 :]
    held_refs, sum_refs, got, sent = refs[:n], refs[n : n + 3], refs[n + 3], refs[n + 4]
    fetch = [pltpu.make_async_copy(a, b, got.at[i]) for i, (a, b) in enumerate(zip(row_refs, held_refs))]
    for copy in fetch:
        copy.start()
    tiles = col_ref[:, 3 * NH * HSZ :].astype(F32)
    gw_ref[...] = jnp.sum(tiles.reshape(POS, OFF, HSZ), axis=0)
    copies = []
    for r, (start, steps) in enumerate(RUNS):
        fetch[r].wait()
        for i in range(3):
            for h in range(start, start + steps):
                at, near = (3 * h + i) * HSZ, (3 * (h - start) + i) * HSZ
                x = held_refs[r][:, near : near + HSZ] + col_ref[:, at : at + HSZ].astype(F32)
                sum_refs[i][:, h * HSZ : (h + 1) * HSZ] = x.astype(BF16)
            at = slice(start * HSZ, (start + steps) * HSZ)
            copies.append(pltpu.make_async_copy(sum_refs[i].at[:, at], out_refs[i].at[:, at], sent.at[3 * r + i]))
            copies[-1].start()
    for copy in copies:
        copy.wait()


def heads(at=0, rows=STRIDE, width=HSZ):
    return pl.BlockSpec((rows, width), lambda h: (0, at + h))


def whole(*shape):
    return pl.BlockSpec(shape, lambda h: (0,) * len(shape))


SMEM = pl.BlockSpec(memory_space=pltpu.SMEM)
PARAMS = pltpu.CompilerParams(vmem_limit_bytes=VMEM, dimension_semantics=("arbitrary",))


def shape(*dims, dtype=F32):
    return jax.ShapeDtypeStruct(dims, dtype)


def hbm(*dims, dtype=F32):
    return pltpu.HBM(dims, dtype)


def cost(us):
    return pl.CostEstimate(flops=int(us * 1e9), bytes_accessed=0, transcendentals=0)


def call(kernel, steps, ins, outs, out_shape, scratch=(), name=None, us=1):
    return pl.pallas_call(
        kernel,
        cost_estimate=cost(us),
        grid=(steps,),
        in_specs=ins,
        out_specs=outs,
        out_shape=out_shape,
        scratch_shapes=list(scratch),
        compiler_params=PARAMS,
        name=name,
    )


def in_hbm(x):
    return pltpu.with_memory_space_constraint(x, pltpu.HBM)


def single(kernel, held, args, out_shape, scratch=(), name=None, out_specs=None, far=(), us=1):
    vmem = pl.BlockSpec(memory_space=pltpu.VMEM)
    return pl.pallas_call(
        kernel,
        cost_estimate=cost(us),
        in_specs=[vmem] * (len(held) + len(args)) + [pl.BlockSpec(memory_space=pltpu.HBM)] * len(far),
        out_specs=jax.tree.map(lambda _: vmem, out_shape) if out_specs is None else out_specs,
        out_shape=out_shape,
        scratch_shapes=list(scratch),
        compiler_params=pltpu.CompilerParams(vmem_limit_bytes=SMALL_VMEM),
        name=name,
    )(*[pltpu.with_memory_space_constraint(x, pltpu.VMEM) for x in held], *args, *[in_hbm(x) for x in far])


def exchange(*arrays):
    x = jnp.concatenate(arrays, axis=1)
    x = lax.all_to_all(x.reshape(POS, OFF, x.shape[1]), "seq", 0, 0, tiled=True)
    return x.reshape(STRIDE, x.shape[2])


def body(queries, keys, values_in, cotangent, w_value, returns):
    seq = lax.axis_size("seq")
    at = lax.axis_index("seq")
    bias = jnp.where(jnp.stack([at == 0, at == seq - 1]), NEG, 0.0).astype(F32)
    w8 = jnp.broadcast_to(w_value[None, :], (8, w_value.shape[0]))
    ret8 = jnp.broadcast_to(returns[None, :], (8, STRIDE))

    got = exchange(queries, keys, values_in, cotangent)
    ahead = [(i, i + 1) for i in range(seq - 1)]
    behind = [(i + 1, i) for i in range(seq - 1)]
    def pair(start, n):
        at = slice(start * HSZ, (start + n) * HSZ)
        return jnp.concatenate([keys[:, at], values_in[:, at]], axis=1)

    pairs = [pair(*r) for r in RUNS]
    *pairs[1:], _ = lax.optimization_barrier((*pairs[1:], got))
    prev = [lax.ppermute(x, "seq", ahead) for x in pairs]
    after = [lax.ppermute(x, "seq", behind) for x in (queries, cotangent)]
    def row_stats(kernel, run, ins, args, name, us, more=(), more_shapes=(), scratch=()):
        n = run[1]
        return call(
            kernel,
            n,
            ins,
            [pl.BlockSpec((HSZ, STRIDE), lambda h: (h, 0)), *more],
            [shape(n * HSZ, STRIDE, dtype=BF16), *more_shapes],
            scratch,
            name,
            us * n,
        )(*args)

    def stat_out(n):
        return [pl.BlockSpec((8, STRIDE), lambda h: (h, 0))], [shape(8 * n, STRIDE)]

    o_own, st_own = row_stats(
        row_own_kernel, (0, NH), [heads()] * 4 + [heads(rows=8)], (queries, keys, values_in, cotangent, w8),
        "row_own", 1, *stat_out(NH),
    )
    w8, ret8, st_own = lax.optimization_barrier((w8, ret8, st_own))
    col_nat, col_pack = single(col_fwd_kernel, (got,), (w8,), [hbm(16, STRIDE), hbm(POS, 128)], name="col_fwd", us=4)
    w8, col_nat, col_pack = lax.optimization_barrier((w8, col_nat, col_pack))
    done, row_o = [], [o_own]
    for (start, n), kv in zip(RUNS, prev):
        there = heads(start)
        ins = [SMEM, there, heads(), heads(n), there, heads(start, rows=8)]
        args = (bias, queries, kv, kv, cotangent, w8)
        if start + n < NH:
            o, st = row_stats(row_cross_kernel, (start, n), ins, args, "row_prev", 1.5, *stat_out(n))
            done.append(st)
        else:
            ins += [whole(8 * m, STRIDE) for _, m in RUNS[:-1]]
            ins += [whole(8 * NH, STRIDE), whole(8, STRIDE), whole(POS, 128)]
            o, row_nat, stats = row_stats(
                row_last_kernel, (start, n), ins, args + (*done, st_own, ret8, col_pack), "row_last", 2,
                [whole(32, STRIDE), whole(POS, 4, 128)], [shape(32, STRIDE), shape(POS, 4, 128)],
                [pltpu.VMEM((8 * n, STRIDE), F32)],
            )
        row_o.append(o)
    stats, next_q, next_c = lax.optimization_barrier((stats, *after))
    stats = lax.all_to_all(stats, "seq", 0, 0, tiled=True)
    next_nat = lax.ppermute(row_nat, "seq", behind)
    t, tc, tn, part = single(
        merge_kernel,
        (stats,),
        (row_nat, next_nat, col_nat),
        [shape(32, STRIDE), shape(16, STRIDE), hbm(16, STRIDE), shape(8, STRIDE)],
        name="merge",
    )
    size = lax.axis_size("head")
    parts = [part] + [lax.ppermute(part, "head", [(i, i ^ d) for i in range(size)]) for d in (1, 2, 3)]

    back_width = 3 * NH * HSZ + HSZ
    col_out, crit = single(
        col_bwd_kernel,
        (got,),
        (w8, tc, t, *parts),
        [hbm(STRIDE, back_width, dtype=BF16), hbm(8, STRIDE)],
        [
            pltpu.VMEM((STRIDE, back_width), BF16),
            pltpu.VMEM((QB, 2 * HSZ), F32),
            pltpu.VMEM((QB, HSZ), F32),
            pltpu.VMEM((2 * NH * HSZ, STRIDE), BF16),
            pltpu.SemaphoreType.DMA((NH + 1 + len(O_RUNS),)),
        ],
        "col_bwd",
        [pl.BlockSpec(memory_space=pltpu.HBM), pl.BlockSpec(memory_space=pltpu.VMEM)],
        row_o,
    )
    back = lax.all_to_all(col_out.reshape(POS, OFF, back_width), "seq", 0, 0, tiled=True)
    back = back.reshape(STRIDE, back_width)

    row_out = []
    for (start, steps), kv in zip(RUNS, prev):
        there = heads(start)
        row_out.append(
            call(
                functools.partial(row_bwd_kernel, start=start),
                steps,
                [SMEM, there, there, heads(), there, heads(steps), there, there, there, heads(start, rows=8)]
                + [whole(32, STRIDE), whole(16, STRIDE), whole(8, STRIDE)],
                heads(width=3 * HSZ),
                shape(STRIDE, 3 * steps * HSZ),
                [
                    pltpu.VMEM((2, STRIDE, HSZ), BF16),
                    pltpu.VMEM((STRIDE, 2 * HSZ), F32),
                    pltpu.VMEM((STRIDE, HSZ), F32),
                ],
                "row_bwd",
                3 * steps,
            )(bias, queries, next_q, kv, keys, kv, values_in, cotangent, next_c, w8, t, tn, crit)
        )

    far, vmem = pl.BlockSpec(memory_space=pltpu.HBM), pl.BlockSpec(memory_space=pltpu.VMEM)
    sums = [pltpu.VMEM((STRIDE, NH * HSZ), BF16)] * 3
    grad_q, grad_k, grad_v, grad_w = pl.pallas_call(
        final_kernel,
        in_specs=[vmem] + [far] * len(RUNS),
        out_specs=[far] * 3 + [vmem],
        out_shape=[hbm(STRIDE, NH * HSZ, dtype=BF16)] * 3 + [shape(8, HSZ)],
        scratch_shapes=[pltpu.VMEM((STRIDE, 3 * n * HSZ), F32) for _, n in RUNS]
        + sums
        + [pltpu.SemaphoreType.DMA((len(RUNS),)), pltpu.SemaphoreType.DMA((3 * len(RUNS),))],
        compiler_params=pltpu.CompilerParams(vmem_limit_bytes=SMALL_VMEM),
        name="final_sum",
    )(pltpu.with_memory_space_constraint(back, pltpu.VMEM), *[in_hbm(x) for x in row_out])
    return crit[0], grad_w[0:NH].reshape(NH * HSZ), grad_q, grad_k, grad_v


def solution(mesh):
    return jax.shard_map(
        body,
        mesh=mesh,
        in_specs=(
            P("seq", "head"),
            P("seq", "head"),
            P("seq", "head"),
            P("seq", "head"),
            P("head"),
            P("seq"),
        ),
        out_specs=(P("seq"), P("head"), P("seq", "head"), P("seq", "head"), P("seq", "head")),
        check_vma=False,
    )
```

```python
import functools

import jax
import jax.numpy as jnp
from jax import lax
from jax.experimental import pallas as pl
from jax.experimental.pallas import tpu as pltpu
from jax.sharding import PartitionSpec as P

HSZ = 128
STRIDE = 512
NH = 5
RUNS = ((0, 2), (2, 2), (4, 1))
O_RUNS = ((0, 5),) + tuple((NH + at, n) for at, n in RUNS)
POS = 64
OFF = 8
QB = 256
NEG = -1e30
SCALE = HSZ ** (-0.5)
VMEM = 60 * 1024 * 1024
SMALL_VMEM = 32 * 1024 * 1024
F32 = jnp.float32
BF16 = jnp.bfloat16


def iota(shape, dim):
    return lax.broadcasted_iota(jnp.int32, shape, dim)


def dot_nt(a, b):
    return lax.dot_general(a, b, (((1,), (1,)), ((), ())), preferred_element_type=F32)


def dot_nn(a, b):
    return lax.dot_general(a, b, (((1,), (0,)), ((), ())), preferred_element_type=F32)


def dot_tn(a, b):
    return lax.dot_general(a, b, (((0,), (0,)), ((), ())), preferred_element_type=F32)


def exact(a, b, dims):
    return lax.dot_general(
        a, b, (dims, ((), ())), preferred_element_type=F32, precision=lax.Precision.HIGHEST
    )


def pack(r):
    spread = (iota((16, 128), 1) // OFF == iota((16, 128), 0)).astype(F32)
    a = exact(r, spread, ((0,), (0,)))
    a = jnp.where(iota((512, 128), 0) % OFF == iota((512, 128), 1) % OFF, a, 0.0)
    gather = (iota((POS, 512), 1) // OFF == iota((POS, 512), 0)).astype(F32)
    return exact(gather, a, ((1,), (0,)))


def unpack(m):
    spread = (iota((512, POS), 0) // OFF == iota((512, POS), 1)).astype(F32)
    a = exact(spread, m, ((1,), (0,)))
    a = jnp.where(iota((512, 128), 0) % OFF == iota((512, 128), 1) % OFF, a, 0.0)
    gather = (iota((16, 128), 1) // OFF == iota((16, 128), 0)).astype(F32)
    return exact(gather, a, ((1,), (1,)))


def split3(x):
    hi = x.astype(BF16)
    rest = x - hi.astype(F32)
    mid = rest.astype(BF16)
    return hi, mid, (rest - mid.astype(F32)).astype(BF16)


def resid_columns(resid):
    hi, mid, lo = split3(resid)
    rows = jnp.concatenate([hi, mid, lo, jnp.zeros((13, 512), BF16)], axis=0)
    eye = (iota((16, 128), 0) == iota((16, 128), 1)).astype(BF16)
    return dot_tn(rows, eye).astype(BF16)


def col_masks():
    token, lane = iota((STRIDE, HSZ), 0), iota((STRIDE, HSZ), 1)
    off, pos = token % OFF, token // OFF
    is_off, is_pos = lane < OFF, (lane >= OFF) & (lane < OFF + POS)
    ka = (is_off & (lane == off)) | (is_pos & (lane - OFF == pos))
    qa = (is_off & (lane != off)) | (is_pos & (lane - OFF >= pos))
    return jnp.where(ka, 1.0, 0.0).astype(BF16), jnp.where(qa, -(2.0**100), 0.0).astype(BF16)


def col_scores(k, q, masks, qb):
    rows, at = slice(0, (qb + 1) * QB), slice(qb * QB, (qb + 1) * QB)
    kx = jnp.concatenate([k[rows], masks[0][rows]], axis=1)
    return dot_nt(kx, jnp.concatenate([q[at], masks[1][at]], axis=1))


def rsum(x):
    return jnp.sum(x, axis=0, keepdims=True)


def stats_of(s, dp, wv):
    top = jnp.max(s, axis=0, keepdims=True)
    e = jnp.exp((s - top) * SCALE)
    z = rsum(e)
    u = rsum(e * wv)
    c = rsum(e * dp)
    m = top * SCALE
    return m + jnp.log(z), u / z, c / z, m, e


def wv_of(v, w):
    return jnp.sum(v.astype(F32) * w, axis=1, keepdims=True)


def row_window(kp_ref, k_ref, qb):
    runs = [kp_ref[0:QB, :], kp_ref[QB:, :], k_ref[0:QB, :], k_ref[QB:, :]]
    return jnp.concatenate(runs[qb : qb + 3], axis=0)


def upper():
    return iota((QB, QB), 0) > iota((QB, QB), 1)


def row_scores(kw, q, bias, qb):
    s = dot_nt(kw, q)
    up = upper()
    s0 = jnp.where(up, s[0:QB], NEG) + bias
    s1 = s[QB : 2 * QB]
    if qb == 0:
        s1 = s1 + bias
    s2 = jnp.where(up, NEG, s[2 * QB :])
    return jnp.concatenate([s0, s1, s2], axis=0)


def put_stats(at, s, dp, v, w, st_ref, o_ref):
    lse, u, c, m, e = stats_of(s, dp, wv_of(v, w))
    o_ref[:, at] = dot_tn(v, e.astype(BF16)).astype(BF16)
    st_ref[:, at] = jnp.concatenate([lse, u, c, m, m, m, m, m], axis=0)


def row_own_kernel(q_ref, k_ref, v_ref, c_ref, w_ref, o_ref, st_ref):
    for qb in range(2):
        at, rows = slice(qb * QB, (qb + 1) * QB), (qb + 1) * QB
        s = dot_nt(k_ref[0:rows, :], q_ref[at, :])
        last = jnp.where(upper(), NEG, s[qb * QB :])
        s = jnp.concatenate([s[0:QB], last], axis=0) if qb else last
        put_stats(at, s, dot_nt(v_ref[0:rows, :], c_ref[at, :]), v_ref[0:rows, :], w_ref[0:1, :], st_ref, o_ref)


def cross_scores(k_ref, qn_ref, bias, qb):
    s = dot_nt(k_ref[qb * QB :, :], qn_ref[qb * QB : (qb + 1) * QB, :]) + bias
    first = jnp.where(upper(), s[0:QB], NEG)
    return first if qb else jnp.concatenate([first, s[QB:]], axis=0)


def row_cross_kernel(bias_ref, q_ref, k_ref, v_ref, c_ref, w_ref, o_ref, st_ref):
    for qb in range(2):
        at = slice(qb * QB, (qb + 1) * QB)
        s = cross_scores(k_ref, q_ref, bias_ref[0], qb)
        v = v_ref[qb * QB :, :]
        put_stats(at, s, dot_nt(v, c_ref[at, :]), v, w_ref[0:1, :], st_ref, o_ref)


def log_add(x, y):
    top = jnp.maximum(x, y)
    return top + jnp.log(jnp.exp(x - top) + jnp.exp(y - top))


def row_last_kernel(*refs):
    *ins, own_ref, ret_ref, col_ref = refs[: 8 + len(RUNS)]
    ins, done = ins[:6], ins[6:]
    o_ref, nat_ref, stats_ref, st_ref = refs[8 + len(RUNS) :]
    h = pl.program_id(0)
    row_cross_kernel(*ins, o_ref, st_ref.at[pl.ds(pl.multiple_of(8 * h, 8), 8)])

    @pl.when(h == RUNS[-1][1] - 1)
    def _():
        cross = [ref[8 * g : 8 * g + 8, :] for (_, n), ref in zip(RUNS, done + [st_ref]) for g in range(n)]
        own = [own_ref[8 * g : 8 * g + 8, :] for g in range(NH)]

        def rows(parts, i):
            return jnp.concatenate([x[i : i + 1] for x in parts], axis=0)

        lse_o, lse_p = rows(own, 0), rows(cross, 0)
        lse = log_add(lse_o, lse_p)
        a_o, a_p = jnp.exp(lse_o - lse), jnp.exp(lse_p - lse)
        u, c = (a_o * rows(own, i) + a_p * rows(cross, i) for i in (1, 2))
        r = jnp.concatenate([lse, u, c, ret_ref[0:1, :]], axis=0)
        nat_ref[0:16, :] = r
        nat_ref[16:32, :] = jnp.concatenate([rows(own, 3), rows(cross, 3), jnp.zeros((6, STRIDE), F32)], axis=0)
        col = col_ref[...]
        stats_ref[:, 0, :] = pack(r)
        stats_ref[:, 1, :] = col
        stats_ref[:, 2, :] = jnp.concatenate([col[1:], jnp.zeros((1, 128), F32)], axis=0)
        stats_ref[:, 3, :] = jnp.zeros((POS, 128), F32)


def col_heads(got_ref, h):
    return (got_ref[:, (i * NH + h) * HSZ : (i * NH + h + 1) * HSZ] for i in range(4))


def col_fwd_kernel(got_ref, w_ref, nat_ref, out_ref):
    masks = col_masks()
    has = iota((1, STRIDE), 1) >= OFF
    rows = [[], [], []]
    for h in range(NH):
        q, k, v, c = col_heads(got_ref, h)
        wv = wv_of(v, w_ref[0:1, h * HSZ : (h + 1) * HSZ])
        parts = []
        for qb in range(2):
            s = col_scores(k, q, masks, qb)
            dp = dot_nt(v[0 : (qb + 1) * QB], c[qb * QB : (qb + 1) * QB])
            parts.append(stats_of(s, dp, wv[0 : (qb + 1) * QB])[0:3])
        for i in range(3):
            row = jnp.concatenate([parts[0][i], parts[1][i]], axis=1)
            rows[i].append(jnp.where(has, row, NEG if i == 0 else 0.0))
    r = jnp.concatenate(rows[0] + rows[1] + rows[2] + [jnp.zeros((1, STRIDE), F32)], axis=0)
    nat_ref[...] = r
    mine = pack(r)
    out_ref[...] = mine


def merge(r, c):
    lse_r, lse_c = r[0:5], c[0:5]
    lse = log_add(lse_r, lse_c)
    a_r, a_c = jnp.exp(lse_r - lse), jnp.exp(lse_c - lse)
    u = a_r * r[5:10] + a_c * c[5:10]
    cc = a_r * r[10:15] + a_c * c[10:15]
    return jnp.concatenate([lse, u, cc, r[15:16]], axis=0), jnp.sum(u, axis=0, keepdims=True)


def merge_kernel(got_ref, rnat_ref, rnext_ref, cnat_ref, t_ref, tc_ref, tn_ref, part_ref):
    nat = rnat_ref[...]
    t, part = merge(nat[0:16], unpack(got_ref[:, 1, :]))
    weight = jnp.exp(nat[16 : 16 + 2 * NH] - jnp.concatenate([t[0:NH], t[0:NH]], axis=0))
    t_ref[0:16, :] = t
    t_ref[16:32, :] = jnp.concatenate([weight, jnp.zeros((16 - 2 * NH, STRIDE), F32)], axis=0)
    tc_ref[...], partc = merge(unpack(got_ref[:, 0, :]), cnat_ref[...])
    tn_ref[...], partn = merge(rnext_ref[0:16, :], unpack(got_ref[:, 2, :]))
    part_ref[...] = jnp.concatenate([part, partc, partn, jnp.zeros((5, STRIDE), F32)], axis=0)


def resid_of(t_ref, crit, role):
    return crit[role : role + 1] - t_ref[15:16, :]


def bwd_lanes(t_ref, resid, h):
    lse = t_ref[pl.ds(h, 1), :]
    u = t_ref[pl.ds(NH + h, 1), :]
    c = t_ref[pl.ds(2 * NH + h, 1), :]
    return lse, c + resid * u


def grads(s, dp, wv, lse, resid, dsum):
    p = jnp.exp(s * SCALE - lse)
    g = p * (dp + (wv * resid - dsum))
    return p.astype(BF16), g.astype(BF16)


def col_bwd_kernel(
    got_ref, w_ref, tc_ref, t_ref, p0_ref, p1_ref, p2_ref, p3_ref, *refs
):
    *o_refs, hbm_ref, crit_ref, out_ref, dv_ref, dk_ref, held_ref, sems = refs
    fetch = [
        pltpu.make_async_copy(ref, held_ref.at[at * HSZ : (at + n) * HSZ], sems.at[NH + 1 + i])
        for i, ((at, n), ref) in enumerate(zip(O_RUNS, o_refs))
    ]
    for copy in fetch:
        copy.start()

    def send(i, width):
        at = slice(i * 3 * HSZ, i * 3 * HSZ + width)
        copy = pltpu.make_async_copy(out_ref.at[:, at], hbm_ref.at[:, at], sems.at[i])
        copy.start()
        return copy

    copies = []
    masks = col_masks()
    crit = (p0_ref[...] + p1_ref[...]) + (p2_ref[...] + p3_ref[...])
    crit_ref[...] = crit
    resid = resid_of(tc_ref, crit, 1)
    rc = resid_columns(resid)
    resid_r = resid_of(t_ref, crit, 0)
    gws = []
    for h in range(NH):
        q, k, v, c = col_heads(got_ref, h)
        w = w_ref[0:1, h * HSZ : (h + 1) * HSZ]
        wv = wv_of(v, w)
        lse, dsum = bwd_lanes(tc_ref, resid, h)
        at_q, at_k, at_v = (slice((3 * h + i) * HSZ, (3 * h + i + 1) * HSZ) for i in range(3))
        for qb in range(2):
            at = slice(qb * QB, (qb + 1) * QB)
            rows = (qb + 1) * QB
            s = col_scores(k, q, masks, qb)
            dp = dot_nt(v[0:rows], c[at])
            p, g = grads(s, dp, wv[0:rows], lse[:, at], resid[:, at], dsum[:, at])
            dv = dot_nn(p, jnp.concatenate([c[at], rc[at]], axis=1))
            dk = dot_nn(g, q[at])
            out_ref[at, at_q] = (dot_tn(g, k[0:rows]) * SCALE).astype(BF16)
            if qb == 0:
                dv_ref[...] = dv
                dk_ref[...] = dk
            else:
                dv = jnp.concatenate([dv[0:QB] + dv_ref[...], dv[QB:]], axis=0)
                dk = jnp.concatenate([dk[0:QB] + dk_ref[...], dk[QB:]], axis=0)
        cj = jnp.sum(dv[:, HSZ:], axis=1, keepdims=True)
        out_ref[:, at_k] = (dk * SCALE).astype(BF16)
        out_ref[:, at_v] = (dv[:, 0:HSZ] + cj * w).astype(BF16)
        gw = rsum(cj * v.astype(F32))
        gws.append(gw)
        copies.append(send(h, 3 * HSZ))
    for copy in fetch:
        copy.wait()
    for h in range(2 * NH):
        weight = resid_r * t_ref[16 + h : 17 + h, :]
        weight = jnp.concatenate(split3(weight) + (jnp.zeros((13, STRIDE), BF16),), axis=0)
        gws[h % NH] = gws[h % NH] + rsum(dot_nt(weight, held_ref[h * HSZ : (h + 1) * HSZ]))
    tile = jnp.concatenate(gws + [jnp.zeros((3, HSZ), F32)], axis=0)
    tile = jnp.broadcast_to(tile[None], (POS, OFF, HSZ)).reshape(STRIDE, HSZ)
    out_ref[:, 3 * NH * HSZ :] = tile.astype(BF16)
    copies.append(send(NH, HSZ))
    for copy in copies:
        copy.wait()


def row_bwd_kernel(
    bias_ref, q_ref, qn_ref, kp_ref, k_ref, vp_ref, v_ref, c_ref, cn_ref, w_ref, t_ref, tn_ref, crit_ref,
    out_ref, rc_ref, dv_ref, dk_ref, *, start,
):
    step = pl.program_id(0)
    h = start + step
    resid = resid_of(t_ref, crit_ref[...], 0)
    resid_n = resid_of(tn_ref, crit_ref[...], 2)

    @pl.when(step == 0)
    def _():
        rc_ref[0] = resid_columns(resid)
        rc_ref[1] = resid_columns(resid_n)

    lse, dsum = bwd_lanes(t_ref, resid, h)
    lse_n, dsum_n = bwd_lanes(tn_ref, resid_n, h)
    w = w_ref[0:1, :]
    wv = wv_of(v_ref[...], w)
    wvp = wv_of(vp_ref[...], w)
    wvx = jnp.concatenate([wvp, wv], axis=0)
    for qb in range(2):
        at = slice(qb * QB, (qb + 1) * QB)
        kw = row_window(kp_ref, k_ref, qb)
        vw = row_window(vp_ref, v_ref, qb)
        s = row_scores(kw, q_ref[at, :], bias_ref[0], qb)
        dp = dot_nt(vw, c_ref[at, :])
        p, g = grads(s, dp, wvx[qb * QB : (qb + 3) * QB], lse[:, at], resid[:, at], dsum[:, at])
        out_ref[at, 0:HSZ] = (dot_tn(g, kw) * SCALE).astype(BF16)
        own = (2 - qb) * QB
        caug = jnp.concatenate([c_ref[at, :], rc_ref[0, at, :]], axis=1)
        dv = dot_nn(p[own:], caug)
        dk = dot_nn(g[own:], q_ref[at, :])
        if qb == 0:
            dv_ref[0:QB, :] = dv
            dk_ref[0:QB, :] = dk
        else:
            dv_ref[0:QB, :] += dv[0:QB]
            dk_ref[0:QB, :] += dk[0:QB]
            dv_ref[QB:, :] = dv[QB:]
            dk_ref[QB:, :] = dk[QB:]
    for qb in range(2):
        at = slice(qb * QB, (qb + 1) * QB)
        vw = v_ref[qb * QB :, :]
        s = cross_scores(k_ref, qn_ref, bias_ref[1], qb)
        dp = dot_nt(vw, cn_ref[at, :])
        p, g = grads(s, dp, wv[qb * QB :], lse_n[:, at], resid_n[:, at], dsum_n[:, at])
        caug = jnp.concatenate([cn_ref[at, :], rc_ref[1, at, :]], axis=1)
        dv_ref[qb * QB :, :] += dot_nn(p, caug)
        dk_ref[qb * QB :, :] += dot_nn(g, qn_ref[at, :])
    cj = jnp.sum(dv_ref[:, HSZ:], axis=1, keepdims=True)
    out_ref[:, HSZ : 2 * HSZ] = (dk_ref[...] * SCALE).astype(BF16)
    out_ref[:, 2 * HSZ :] = (dv_ref[:, 0:HSZ] + cj * w).astype(BF16)


def final_kernel(col_ref, *refs):
    n = len(RUNS)
    row_refs, out_refs, gw_ref, refs = refs[:n], refs[n : n + 3], refs[n + 3], refs[n + 4 :]
    held_refs, sum_refs, got, sent = refs[:n], refs[n : n + 3], refs[n + 3], refs[n + 4]
    fetch = [pltpu.make_async_copy(a, b, got.at[i]) for i, (a, b) in enumerate(zip(row_refs, held_refs))]
    for copy in fetch:
        copy.start()
    tiles = col_ref[:, 3 * NH * HSZ :].astype(F32)
    tile = jnp.sum(tiles.reshape(POS, OFF, HSZ), axis=0)
    for h in range(NH):
        gw_ref[:, h * HSZ : (h + 1) * HSZ] = tile[h : h + 1]
    copies = []
    for r, (start, steps) in enumerate(RUNS):
        fetch[r].wait()
        for i in range(3):
            for h in range(start, start + steps):
                at, near = (3 * h + i) * HSZ, (3 * (h - start) + i) * HSZ
                x = held_refs[r][:, near : near + HSZ].astype(F32) + col_ref[:, at : at + HSZ].astype(F32)
                sum_refs[i][:, h * HSZ : (h + 1) * HSZ] = x.astype(BF16)
            at = slice(start * HSZ, (start + steps) * HSZ)
            copies.append(pltpu.make_async_copy(sum_refs[i].at[:, at], out_refs[i].at[:, at], sent.at[3 * r + i]))
            copies[-1].start()
    for copy in copies:
        copy.wait()


def heads(at=0, rows=STRIDE, width=HSZ):
    return pl.BlockSpec((rows, width), lambda h: (0, at + h))


def whole(*shape):
    return pl.BlockSpec(shape, lambda h: (0,) * len(shape))


SMEM = pl.BlockSpec(memory_space=pltpu.SMEM)
PARAMS = pltpu.CompilerParams(vmem_limit_bytes=VMEM, dimension_semantics=("arbitrary",))


def shape(*dims, dtype=F32):
    return jax.ShapeDtypeStruct(dims, dtype)


def hbm(*dims, dtype=F32):
    return pltpu.HBM(dims, dtype)


def cost(us):
    return pl.CostEstimate(flops=int(us * 1e9), bytes_accessed=0, transcendentals=0)


def call(kernel, steps, ins, outs, out_shape, scratch=(), name=None, us=1):
    return pl.pallas_call(
        kernel,
        cost_estimate=cost(us),
        grid=(steps,),
        in_specs=ins,
        out_specs=outs,
        out_shape=out_shape,
        scratch_shapes=list(scratch),
        compiler_params=PARAMS,
        name=name,
    )


def in_hbm(x):
    return pltpu.with_memory_space_constraint(x, pltpu.HBM)


def single(kernel, held, args, out_shape, scratch=(), name=None, out_specs=None, far=(), us=1):
    vmem = pl.BlockSpec(memory_space=pltpu.VMEM)
    return pl.pallas_call(
        kernel,
        cost_estimate=cost(us),
        in_specs=[vmem] * (len(held) + len(args)) + [pl.BlockSpec(memory_space=pltpu.HBM)] * len(far),
        out_specs=jax.tree.map(lambda _: vmem, out_shape) if out_specs is None else out_specs,
        out_shape=out_shape,
        scratch_shapes=list(scratch),
        compiler_params=pltpu.CompilerParams(vmem_limit_bytes=SMALL_VMEM),
        name=name,
    )(*[pltpu.with_memory_space_constraint(x, pltpu.VMEM) for x in held], *args, *[in_hbm(x) for x in far])


def exchange(*arrays):
    x = jnp.concatenate(arrays, axis=1)
    x = lax.all_to_all(x.reshape(POS, OFF, x.shape[1]), "seq", 0, 0, tiled=True)
    return x.reshape(STRIDE, x.shape[2])


def body(queries, keys, values_in, cotangent, w_value, returns):
    seq = lax.axis_size("seq")
    at = lax.axis_index("seq")
    bias = jnp.where(jnp.stack([at == 0, at == seq - 1]), NEG, 0.0).astype(F32)
    w8 = jnp.broadcast_to(w_value[None, :], (8, w_value.shape[0]))
    ret8 = jnp.broadcast_to(returns[None, :], (8, STRIDE))

    got = exchange(queries, keys, values_in, cotangent)
    ahead = [(i, i + 1) for i in range(seq - 1)]
    behind = [(i + 1, i) for i in range(seq - 1)]
    def pair(start, n):
        at = slice(start * HSZ, (start + n) * HSZ)
        return jnp.concatenate([keys[:, at], values_in[:, at]], axis=1)

    pairs = [pair(*r) for r in RUNS]
    *pairs[1:], _ = lax.optimization_barrier((*pairs[1:], got))
    prev = [lax.ppermute(x, "seq", ahead) for x in pairs]
    after = [lax.ppermute(x, "seq", behind) for x in (queries, cotangent)]
    def row_stats(kernel, run, ins, args, name, us, more=(), more_shapes=(), scratch=()):
        n = run[1]
        return call(
            kernel,
            n,
            ins,
            [pl.BlockSpec((HSZ, STRIDE), lambda h: (h, 0)), *more],
            [shape(n * HSZ, STRIDE, dtype=BF16), *more_shapes],
            scratch,
            name,
            us * n,
        )(*args)

    def stat_out(n):
        return [pl.BlockSpec((8, STRIDE), lambda h: (h, 0))], [shape(8 * n, STRIDE)]

    o_own, st_own = row_stats(
        row_own_kernel, (0, NH), [heads()] * 4 + [heads(rows=8)], (queries, keys, values_in, cotangent, w8),
        "row_own", 1, *stat_out(NH),
    )
    w8, st_own = lax.optimization_barrier((w8, st_own))
    col_nat, col_pack = single(col_fwd_kernel, (got,), (w8,), [hbm(16, STRIDE), hbm(POS, 128)], name="col_fwd", us=4)
    w8, col_nat, col_pack = lax.optimization_barrier((w8, col_nat, col_pack))
    done, row_o = [], [o_own]
    for (start, n), kv in zip(RUNS, prev):
        there = heads(start)
        ins = [SMEM, there, heads(), heads(n), there, heads(start, rows=8)]
        args = (bias, queries, kv, kv, cotangent, w8)
        if start + n < NH:
            o, st = row_stats(row_cross_kernel, (start, n), ins, args, "row_prev", 1.5, *stat_out(n))
            done.append(st)
        else:
            ins += [whole(8 * m, STRIDE) for _, m in RUNS[:-1]]
            ins += [whole(8 * NH, STRIDE), whole(8, STRIDE), whole(POS, 128)]
            o, row_nat, stats = row_stats(
                row_last_kernel, (start, n), ins, args + (*done, st_own, ret8, col_pack), "row_last", 2,
                [whole(32, STRIDE), whole(POS, 4, 128)], [shape(32, STRIDE), shape(POS, 4, 128)],
                [pltpu.VMEM((8 * n, STRIDE), F32)],
            )
        row_o.append(o)
    stats, next_q, next_c = lax.optimization_barrier((stats, *after))
    stats = lax.all_to_all(stats, "seq", 0, 0, tiled=True)
    next_nat = lax.ppermute(row_nat, "seq", behind)
    t, tc, tn, part = single(
        merge_kernel,
        (stats,),
        (row_nat, next_nat, col_nat),
        [shape(32, STRIDE), shape(16, STRIDE), hbm(16, STRIDE), shape(8, STRIDE)],
        name="merge",
    )
    size = lax.axis_size("head")
    parts = [part] + [lax.ppermute(part, "head", [(i, i ^ d) for i in range(size)]) for d in (1, 2, 3)]

    back_width = 3 * NH * HSZ + HSZ
    col_out, crit = single(
        col_bwd_kernel,
        (got,),
        (w8, tc, t, *parts),
        [hbm(STRIDE, back_width, dtype=BF16), hbm(8, STRIDE)],
        [
            pltpu.VMEM((STRIDE, back_width), BF16),
            pltpu.VMEM((QB, 2 * HSZ), F32),
            pltpu.VMEM((QB, HSZ), F32),
            pltpu.VMEM((2 * NH * HSZ, STRIDE), BF16),
            pltpu.SemaphoreType.DMA((NH + 1 + len(O_RUNS),)),
        ],
        "col_bwd",
        [pl.BlockSpec(memory_space=pltpu.HBM), pl.BlockSpec(memory_space=pltpu.VMEM)],
        row_o,
    )
    back = lax.all_to_all(col_out.reshape(POS, OFF, back_width), "seq", 0, 0, tiled=True)
    back = back.reshape(STRIDE, back_width)

    row_out = []
    for (start, steps), kv in zip(RUNS, prev):
        there = heads(start)
        row_out.append(
            call(
                functools.partial(row_bwd_kernel, start=start),
                steps,
                [SMEM, there, there, heads(), there, heads(steps), there, there, there, heads(start, rows=8)]
                + [whole(32, STRIDE), whole(16, STRIDE), whole(8, STRIDE)],
                heads(width=3 * HSZ),
                shape(STRIDE, 3 * steps * HSZ, dtype=BF16),
                [
                    pltpu.VMEM((2, STRIDE, HSZ), BF16),
                    pltpu.VMEM((STRIDE, 2 * HSZ), F32),
                    pltpu.VMEM((STRIDE, HSZ), F32),
                ],
                "row_bwd",
                3 * steps,
            )(bias, queries, next_q, kv, keys, kv, values_in, cotangent, next_c, w8, t, tn, crit)
        )

    far, vmem = pl.BlockSpec(memory_space=pltpu.HBM), pl.BlockSpec(memory_space=pltpu.VMEM)
    sums = [pltpu.VMEM((STRIDE, NH * HSZ), BF16)] * 3
    grad_q, grad_k, grad_v, grad_w = pl.pallas_call(
        final_kernel,
        in_specs=[vmem] + [far] * len(RUNS),
        out_specs=[far] * 3 + [vmem],
        out_shape=[hbm(STRIDE, NH * HSZ, dtype=BF16)] * 3 + [shape(1, NH * HSZ)],
        scratch_shapes=[pltpu.VMEM((STRIDE, 3 * n * HSZ), BF16) for _, n in RUNS]
        + sums
        + [pltpu.SemaphoreType.DMA((len(RUNS),)), pltpu.SemaphoreType.DMA((3 * len(RUNS),))],
        compiler_params=pltpu.CompilerParams(vmem_limit_bytes=SMALL_VMEM),
        name="final_sum",
    )(pltpu.with_memory_space_constraint(back, pltpu.VMEM), *[in_hbm(x) for x in row_out])
    return crit[0], grad_w.reshape(NH * HSZ), grad_q, grad_k, grad_v


def solution(mesh):
    return jax.shard_map(
        body,
        mesh=mesh,
        in_specs=(
            P("seq", "head"),
            P("seq", "head"),
            P("seq", "head"),
            P("seq", "head"),
            P("head"),
            P("seq"),
        ),
        out_specs=(P("seq"), P("head"), P("seq", "head"), P("seq", "head"), P("seq", "head")),
        check_vma=False,
    )
```
